512 devices in a mesh: dp: 8 (over z), seq: 64 (over y, x, core).
Axes of the slice: x: 4, y: 8, z: 8, core: 2. Of those that a mesh axis runs over, the one named last changes fastest.
Arguments:
- q_raw: bfloat16 [8, 8192, 1536], P('dp', 'seq'), may hold values from -6 to 6
- k_raw: bfloat16 [8, 8192, 1536], P('dp', 'seq'), may hold values from -6 to 6
- values: bfloat16 [8, 8192, 1536], P('dp', 'seq'), may hold values from -6 to 6
- d_out: bfloat16 [8, 8192, 1536], P('dp', 'seq'), may hold values from -6 to 6
- q_gain: float32 [128], replicated, may hold values from 0.1 to 1.9
- k_gain: float32 [128], replicated, may hold values from 0.1 to 1.9
- offsets: int32 [12, 5], replicated, may hold values from 0 to 4, each once within a row
- counts: int32 [128, 12], replicated, may hold values from 1 to 5, as said below
Outputs:
- attn_out: bfloat16 [8, 8192, 1536], P('dp', 'seq')
- q_grad: bfloat16 [8, 8192, 1536], P('dp', 'seq')
- k_grad: bfloat16 [8, 8192, 1536], P('dp', 'seq')
- v_grad: bfloat16 [8, 8192, 1536], P('dp', 'seq')
- q_gain_grad: float32 [128], replicated
- k_gain_grad: float32 [128], replicated
The draws below stay inside these ranges and needn't reach their ends.
Inputs may be any that keep to these rules, and one draw needn't show every extreme that they name: Each row of offsets holds every slot 0 .. 4 once. counts[i, h] is how many leading entries of offsets[h] query tile i of head h uses.
All inputs are finite; a program needn't handle non-finite values.
Results may differ from the reference program's by a relative error of at most 0.01.
Values may be sent and summed in bfloat16 or wider, within the bound.
No kernel may reach another device: no remote copies, remote signals or barrier semaphores. Data moves between devices by JAX's collectives and lax.ppermute only.
A program may use at most 64 MiB of HBM per device.

```python
import jax
import jax.numpy as jnp
from jax import lax

HD = 128
HEADS = 12
HEAD_COLS = 1536
TILE = 64
TILES_DEV = 2
REACH = 2
NOFF = 5
TOKENS = 8192
NTILES = 128
CLIPS = 8


def draw_counts(key, part):
    key = jax.random.fold_in(key, 11)
    key_busy, key_count, key_peak = jax.random.split(key, 3)
    blocks = NTILES // TILES_DEV
    crowded = jax.random.randint(key_busy, (blocks,), 0, 4) == 0
    ceiling = jnp.where(crowded, NOFF + 1, NOFF // 4 + 2)
    ceiling = jnp.repeat(ceiling, TILES_DEV)
    sampled = jax.random.randint(key_count, (NTILES, HEADS), 1, ceiling[:, None])
    chosen = jax.random.randint(key_peak, (HEADS,), 0, NTILES)
    tile_rows = jnp.arange(NTILES)[:, None]
    return jnp.where(tile_rows == chosen[None, :], NOFF, sampled).astype(jnp.int32)


def block_scale(own_key, shape, cuts, least, largest):
    loudness = 1.0
    for dim, shards_of in cuts:
        heights = jax.random.uniform(jax.random.fold_in(jax.random.fold_in(own_key, 6), dim), (shards_of,), jnp.float32, least / len(cuts), largest / len(cuts))
        loudness = loudness * jnp.repeat(jnp.exp(heights), shape[dim] // shards_of).reshape((-1,) + (1,) * (len(shape) - 1 - dim))
    return loudness


def centred(rng, extent, deviation, limit, cuts=(), kind=jnp.bfloat16):
    entries = jax.random.normal(rng, extent, jnp.float32) * deviation
    if len(cuts) > 0:
        entries = block_scale(rng, extent, cuts, -0.22, 0.18) * entries
    return jnp.clip(entries, min=-limit, max=limit).astype(kind)


def setup_inputs(seed: int = 0) -> dict:
    splits = jax.random.split(jax.random.key(seed), 9)
    q_raw = centred(splits[0], (CLIPS, TOKENS, HEAD_COLS), 1.0, 6.0, ((0, 8), (1, 64)))
    k_raw = centred(splits[1], (CLIPS, TOKENS, HEAD_COLS), 1.0, 6.0, ((0, 8), (1, 64)))
    values = centred(splits[2], (CLIPS, TOKENS, HEAD_COLS), 1.0, 6.0, ((0, 8), (1, 64)))
    d_out = centred(splits[3], (CLIPS, TOKENS, HEAD_COLS), 1.0, 6.0, ((0, 8), (1, 64)))
    q_gain = jnp.clip(1.0 + 0.18 * jax.random.normal(splits[4], (HD,), jnp.float32), 0.1, 1.9)
    k_gain = jnp.clip(1.0 + 0.18 * jax.random.normal(splits[5], (HD,), jnp.float32), 0.1, 1.9)
    offsets = jax.vmap(lambda own: jax.random.permutation(own, NOFF))(jax.random.split(splits[6], HEADS)).reshape((HEADS, NOFF)).astype(jnp.int32)
    counts = draw_counts(jax.random.fold_in(splits[8], 71), 0)
    return dict(q_raw=q_raw, k_raw=k_raw, values=values, d_out=d_out, q_gain=q_gain, k_gain=k_gain, offsets=offsets, counts=counts)


def normalize(raw_rows, gain_vec):
    as_float = raw_rows.astype(jnp.float32)
    spread = jnp.sqrt(lax.optimization_barrier(jnp.mean(as_float * as_float, axis=-1, keepdims=True)) + 1e-06)
    unit_rows = as_float / spread
    return (unit_rows, spread, (unit_rows * gain_vec).astype(jnp.bfloat16))

def norm_grad(grad_n, unit_rows, spread, gain_vec):
    scaled = grad_n * gain_vec
    return (scaled - unit_rows * lax.optimization_barrier(jnp.mean(scaled * unit_rows, axis=-1, keepdims=True))) / spread

def reference(q_raw, k_raw, values, d_out, q_gain, k_gain, offsets, counts):
    head_count = offsets.shape[0]
    head_width = q_gain.shape[0]
    ntiles = TOKENS // TILE
    reach_tiles = REACH
    slot_total = NOFF
    score_scale = head_width ** (-0.5)
    slot_ids = jnp.arange(slot_total, dtype=jnp.int32)
    slot_rank = lax.optimization_barrier(jnp.sum(slot_ids[None, :, None] * (offsets[:, :, None] == slot_ids[None, None, :]).astype(jnp.int32), axis=1))
    key_tiles = jnp.arange(ntiles, dtype=jnp.int32)[:, None] + slot_ids[None, :] - reach_tiles
    inside = (key_tiles >= 0) & (key_tiles < ntiles)
    allowed = inside[None] & ((slot_ids == reach_tiles)[None, None, :] | (slot_rank[:, None, :] < counts.T[:, :, None]))

    def windowed(x):
        padded = jnp.pad(x, ((reach_tiles, reach_tiles), (0, 0), (0, 0)))
        stacked = jnp.stack([padded[slot:slot + ntiles] for slot in range(slot_total)], axis=1)
        return stacked.reshape(ntiles, slot_total * TILE, head_width)

    def fold_back(pieces):
        summed = jnp.zeros((ntiles + 2 * reach_tiles, TILE, head_width), jnp.float32)
        for slot in range(slot_total):
            summed = summed.at[slot:slot + ntiles].add(pieces[:, slot])
        return summed[reach_tiles:reach_tiles + ntiles]

    def one_head(head_items):
        q_norm, k_norm, value_rows, grad_rows, allowed_h = head_items
        key_mask = jnp.repeat(allowed_h, TILE, axis=1)
        key_win = windowed(k_norm).astype(jnp.float32)
        value_win = windowed(value_rows).astype(jnp.float32)
        query_f = q_norm.astype(jnp.float32)
        grad_f = grad_rows.astype(jnp.float32)
        scores = jnp.einsum('itd,ikd->itk', query_f, key_win) * score_scale
        scores = jnp.where(key_mask[:, None, :], scores, -jnp.inf)
        row_max = lax.optimization_barrier(jnp.max(scores, axis=-1, keepdims=True))
        log_total = row_max[..., 0] + jnp.log(lax.optimization_barrier(jnp.sum(jnp.exp(scores - row_max), axis=-1)))
        chances = jnp.exp(scores - log_total[..., None])
        weights = chances.astype(jnp.bfloat16)
        attended = jnp.einsum('itk,ikd->itd', weights.astype(jnp.float32), value_win).astype(jnp.bfloat16)
        out_dot = lax.optimization_barrier(jnp.sum(grad_f * attended.astype(jnp.float32), axis=-1))
        grad_prob = jnp.einsum('itd,ikd->itk', grad_f, value_win)
        dscore = (chances * (grad_prob - out_dot[..., None])).astype(jnp.bfloat16)
        dscore_f = dscore.astype(jnp.float32)
        grad_qn = jnp.einsum('itk,ikd->itd', dscore_f, key_win) * score_scale
        grad_kwin = (jnp.einsum('itk,itd->ikd', dscore_f, query_f) * score_scale).reshape(ntiles, slot_total, TILE, head_width)
        grad_vwin = jnp.einsum('itk,itd->ikd', weights.astype(jnp.float32), grad_f).reshape(ntiles, slot_total, TILE, head_width)
        return (attended, grad_qn, fold_back(grad_kwin), fold_back(grad_vwin))

    def to_heads(x):
        return x.reshape(ntiles, TILE, head_count, head_width).transpose(2, 0, 1, 3)

    def from_heads(x):
        return x.transpose(1, 2, 0, 3).reshape(TOKENS, head_count, head_width)

    def one_clip(clip_items):
        clip_q, clip_k, clip_v, clip_g = clip_items
        head_shape = (TOKENS, head_count, head_width)
        q_unit, q_spread, q_norm = normalize(clip_q.reshape(head_shape), q_gain)
        k_unit, k_spread, k_norm = normalize(clip_k.reshape(head_shape), k_gain)
        attended, grad_qn, grad_kn, grad_v = lax.map(one_head, (to_heads(q_norm), to_heads(k_norm), to_heads(clip_v.reshape(head_shape)), to_heads(clip_g.reshape(head_shape)), allowed))
        grad_qn = from_heads(grad_qn)
        grad_kn = from_heads(grad_kn)
        q_grad = norm_grad(grad_qn, q_unit, q_spread, q_gain).astype(jnp.bfloat16)
        k_grad = norm_grad(grad_kn, k_unit, k_spread, k_gain).astype(jnp.bfloat16)
        gain_terms = jnp.stack([lax.optimization_barrier(jnp.sum(grad_qn * q_unit, axis=(0, 1))), lax.optimization_barrier(jnp.sum(grad_kn * k_unit, axis=(0, 1)))])
        flat_cols = head_count * head_width
        return (from_heads(attended).reshape(TOKENS, flat_cols), q_grad.reshape(TOKENS, flat_cols), k_grad.reshape(TOKENS, flat_cols), from_heads(grad_v).astype(jnp.bfloat16).reshape(TOKENS, flat_cols), gain_terms)
    results = lax.map(one_clip, (q_raw, k_raw, values, d_out))
    gain_total = lax.optimization_barrier(jnp.sum(results[4], axis=0))
    return (results[0], results[1], results[2], results[3], gain_total[0], gain_total[1])
```

```python
import math

import jax
import jax.numpy as jnp
from jax import lax
from jax.experimental import pallas as pl
from jax.experimental.pallas import tpu as pltpu
from jax.sharding import PartitionSpec as P

TILE = 64
REACH = 2
EPS = 1e-06
HEADS_PER_STEP = 4
NT = (((1,), (1,)), ((), ()))
NN = (((1,), (0,)), ((), ()))


def dot(a, b, dims):
    return lax.dot_general(a, b, dims, preferred_element_type=jnp.float32)


def inverse_spread(rows, axis):
    return lax.rsqrt(jnp.mean(rows * rows, axis=axis, keepdims=True) + EPS)


def shift(block, distance):
    size = lax.axis_size("seq")
    route = [(i, i + distance) for i in range(size) if 0 <= i + distance < size]
    return lax.ppermute(block, "seq", route)


def prepare_kernel(width, q_ref, k_ref, g_ref, qg_ref, kg_ref, qn_ref, qt_ref, gt_ref, kn_ref, kt_ref):
    q_gain = qg_ref[...]
    k_gain = kg_ref[...]
    for h in range(q_ref.shape[1] // width):
        cols = slice(h * width, (h + 1) * width)
        q = q_ref[:, cols].astype(jnp.float32)
        qn = (q * inverse_spread(q, 1) * q_gain).astype(jnp.bfloat16)
        qn_ref[:, cols] = qn
        qt_ref[cols, :] = qn.T
        gt_ref[cols, :] = g_ref[:, cols].T
        k_raw = k_ref[:, cols]
        k = k_raw.astype(jnp.float32)
        kn_ref[:, cols] = (k * inverse_spread(k, 1) * k_gain).astype(jnp.bfloat16)
        kt_ref[cols, :] = k_raw.T


def attend_kernel(
    width,
    q_ref,
    qn_ref,
    qt_ref,
    g_ref,
    gt_ref,
    kn_ref,
    v_ref,
    low_ref,
    high_ref,
    mask_ref,
    qg_ref,
    kg_ref,
    out_ref,
    qgrad_ref,
    own_ref,
    to_low_ref,
    to_high_ref,
    gain_ref,
):
    q_gain = qg_ref[...]
    k_gain = kg_ref[...]
    rows = q_ref.shape[0]
    scale = width ** (-0.5)
    gain_sum = jnp.zeros((rows, width), jnp.float32)
    for h in range(q_ref.shape[1] // width):
        cols = slice(h * width, (h + 1) * width)

        def normal(raw):
            x = raw.astype(jnp.float32)
            return (x * inverse_spread(x, 1) * k_gain).astype(jnp.bfloat16)

        keys = jnp.concatenate(
            [normal(low_ref[0, :, cols]), kn_ref[:, cols], normal(high_ref[0, :, cols])], axis=0
        )
        vals = jnp.concatenate([low_ref[1, :, cols], v_ref[:, cols], high_ref[1, :, cols]], axis=0)
        mask = jnp.concatenate(
            [
                jnp.broadcast_to(mask_ref[h, t : t + 1, :], (TILE, 3 * rows))
                for t in range(rows // TILE)
            ],
            axis=0,
        )
        grads = g_ref[:, cols]
        scores = dot(qn_ref[:, cols], keys, NT)
        terms = jnp.exp2(scores * (scale * math.log2(math.e))) * mask
        probs = terms * (1.0 / jnp.sum(terms, axis=1, keepdims=True))
        weights = probs.astype(jnp.bfloat16)
        dprob = dot(grads, vals, NT)
        delta = jnp.sum(probs * dprob, axis=1, keepdims=True)
        dscore = (probs * (dprob - delta)).astype(jnp.bfloat16)
        out_ref[:, cols] = dot(weights, vals, NN).astype(jnp.bfloat16)
        grad_qn = dot(dscore, keys, NN) * scale
        key_t = dot(qt_ref[cols, :], dscore, NN) * scale
        val_t = dot(gt_ref[cols, :], weights, NN)
        own_ref[0, cols, :] = key_t[:, rows : 2 * rows]
        own_ref[1, cols, :] = val_t[:, rows : 2 * rows]
        to_low_ref[0, cols, :] = key_t[:, :rows].astype(jnp.bfloat16)
        to_low_ref[1, cols, :] = val_t[:, :rows].astype(jnp.bfloat16)
        to_high_ref[0, cols, :] = key_t[:, 2 * rows :].astype(jnp.bfloat16)
        to_high_ref[1, cols, :] = val_t[:, 2 * rows :].astype(jnp.bfloat16)
        q = q_ref[:, cols].astype(jnp.float32)
        inverse = inverse_spread(q, 1)
        unit = q * inverse
        product = grad_qn * unit
        gain_sum = gain_sum + product
        mean = jnp.mean(product * q_gain, axis=1, keepdims=True)
        qgrad_ref[:, cols] = ((grad_qn * q_gain - unit * mean) * inverse).astype(jnp.bfloat16)

    @pl.when(pl.program_id(0) == 0)
    def _():
        gain_ref[...] = jnp.zeros_like(gain_ref)

    gain_ref[...] += jnp.sum(gain_sum, axis=0, keepdims=True)


def finish_kernel(width, kt_ref, own_ref, low_ref, high_ref, kg_ref, kgrad_ref, vgrad_ref):
    gain = kg_ref[...]
    for h in range(kgrad_ref.shape[1] // width):
        cols = slice(h * width, (h + 1) * width)

        def total(i):
            return (
                own_ref[i, cols, :]
                + low_ref[i, cols, :].astype(jnp.float32)
                + high_ref[i, cols, :].astype(jnp.float32)
            )

        k = kt_ref[cols, :].astype(jnp.float32)
        inverse = inverse_spread(k, 0)
        unit = k * inverse
        scaled = total(0) * gain
        mean = jnp.mean(scaled * unit, axis=0, keepdims=True)
        kgrad_ref[:, cols] = ((scaled - unit * mean) * inverse).astype(jnp.bfloat16).T
        vgrad_ref[:, cols] = total(1).astype(jnp.bfloat16).T


def window_mask(offsets, counts, tiles_here):
    heads, slots = offsets.shape
    ntiles = counts.shape[0]
    first = lax.axis_index("seq") * tiles_here
    slot = jnp.arange(slots, dtype=jnp.int32)
    rank = jnp.sum(slot[None, :, None] * (offsets[:, :, None] == slot[None, None, :]), axis=1)
    used = lax.dynamic_slice_in_dim(counts, first, tiles_here, axis=0).T
    query = first + jnp.arange(tiles_here, dtype=jnp.int32)
    key = query[:, None] + slot[None, :] - REACH
    inside = (key >= 0) & (key < ntiles)
    allowed = inside[None] & ((slot == REACH)[None, None] | (rank[:, None, :] < used[:, :, None]))
    allowed = allowed.astype(jnp.float32)
    rows = [
        jnp.pad(allowed[:, t], ((0, 0), (t, tiles_here - 1 - t))) for t in range(tiles_here)
    ]
    return jnp.repeat(jnp.stack(rows, axis=1), TILE, axis=2)


def call(body, grid, in_specs, out_specs, out_shape, flops):
    return pl.pallas_call(
        body,
        grid=grid,
        in_specs=in_specs,
        out_specs=out_specs,
        out_shape=out_shape,
        compiler_params=pltpu.CompilerParams(vmem_limit_bytes=32 * 1024 * 1024),
        cost_estimate=pl.CostEstimate(flops=flops, bytes_accessed=4 << 20, transcendentals=0),
    )


def total_over(axis, vector):
    size = lax.axis_size(axis)
    spread = jnp.broadcast_to(vector[None], (size,) + vector.shape)
    return jnp.sum(lax.all_to_all(spread, axis, 0, 0), axis=0)


def shards(q_raw, k_raw, values, d_out, q_gain, k_gain, offsets, counts):
    rows, columns = q_raw.shape[1:]
    width = q_gain.shape[0]
    heads = offsets.shape[0]
    step = min(HEADS_PER_STEP, heads)
    chunk = step * width
    grid = (heads // step,)
    key_value = jnp.concatenate([k_raw, values], axis=0)
    low = shift(key_value, 1)
    high = shift(key_value, -1)
    q, k, v, g = q_raw[0], k_raw[0], values[0], d_out[0]
    q_row, k_row = q_gain[None], k_gain[None]
    mask = window_mask(offsets, counts, rows // TILE)

    flat = pl.BlockSpec((rows, chunk), lambda j: (0, j))
    turned = pl.BlockSpec((chunk, rows), lambda j: (j, 0))
    pair = pl.BlockSpec((2, rows, chunk), lambda j: (0, 0, j))
    turned_pair = pl.BlockSpec((2, chunk, rows), lambda j: (0, j, 0))
    vector = pl.BlockSpec((1, width), lambda j: (0, 0))
    flat_shape = jax.ShapeDtypeStruct((rows, columns), jnp.bfloat16)
    turned_shape = jax.ShapeDtypeStruct((columns, rows), jnp.bfloat16)
    part_shape = jax.ShapeDtypeStruct((2, columns, rows), jnp.bfloat16)

    def prepare(*refs):
        prepare_kernel(width, *refs)

    def attend(*refs):
        attend_kernel(width, *refs)

    def finish(*refs):
        finish_kernel(width, *refs)

    qn, qt, gt, kn, kt = call(
        prepare,
        grid,
        [flat, flat, flat, vector, vector],
        [flat, turned, turned, flat, turned],
        [flat_shape, turned_shape, turned_shape, flat_shape, turned_shape],
        rows * columns * 40,
    )(q, k, g, q_row, k_row)
    out, q_grad, own, to_low, to_high, gain = call(
        attend,
        grid,
        [flat, flat, turned, flat, turned, flat, flat, pair, pair]
        + [pl.BlockSpec((step, rows // TILE, 3 * rows), lambda j: (j, 0, 0)), vector, vector],
        [flat, flat, turned_pair, turned_pair, turned_pair, vector],
        [
            flat_shape,
            flat_shape,
            jax.ShapeDtypeStruct((2, columns, rows), jnp.float32),
            part_shape,
            part_shape,
            jax.ShapeDtypeStruct((1, width), jnp.float32),
        ],
        rows * rows * columns * 36,
    )(q, qn, qt, g, gt, kn, v, low, high, mask, q_row, k_row)
    from_high = shift(to_low, -1)
    from_low = shift(to_high, 1)
    gain = total_over("dp", total_over("seq", gain))[0]
    k_grad, v_grad = call(
        finish,
        grid,
        [turned, turned_pair, turned_pair, turned_pair, pl.BlockSpec((width, 1), lambda j: (0, 0))],
        [flat, flat],
        [flat_shape, flat_shape],
        rows * columns * 40,
    )(kt, own, from_low, from_high, k_gain[:, None])
    return (
        out[None],
        q_grad[None],
        k_grad[None],
        v_grad[None],
        gain,
        gain * q_gain / k_gain,
    )


def solution(mesh):
    tokens = P("dp", "seq", None)
    return jax.shard_map(
        shards,
        mesh=mesh,
        in_specs=(tokens, tokens, tokens, tokens, P(), P(), P(), P()),
        out_specs=(tokens, tokens, tokens, tokens, P(), P()),
        check_vma=False,
    )
```

```python
import math

import jax
import jax.numpy as jnp
from jax import lax
from jax.experimental import pallas as pl
from jax.experimental.pallas import tpu as pltpu
from jax.sharding import PartitionSpec as P

TILE = 64
REACH = 2
EPS = 1e-06
GROUP = 6
STEP = 3
NT = (((1,), (1,)), ((), ()))
NN = (((1,), (0,)), ((), ()))
F32 = jnp.float32
BF16 = jnp.bfloat16


def dot(a, b, dims):
    return lax.dot_general(a, b, dims, preferred_element_type=F32)


def inverse_spread(rows, axis):
    return lax.rsqrt(jnp.mean(rows * rows, axis=axis, keepdims=True) + EPS)


def swap(block, parity):
    size = lax.axis_size("seq")
    route = [(i, i + 1 if i % 2 == parity else i - 1) for i in range(size)]
    return lax.ppermute(block, "seq", [(i, j) for i, j in route if 0 <= j < size])


def head_columns(ref, width):
    return [slice(h * width, (h + 1) * width) for h in range(ref.shape[-1] // width)]


def window_mask(offsets_t, counts_t, position, t, rows):
    slots, heads = offsets_t.shape
    ntiles = counts_t.shape[1]
    tiles = rows // TILE
    lane = lax.broadcasted_iota(jnp.int32, (heads, 3 * rows), 1)
    side = 1 - 2 * lax.rem(position, 2)
    block = (lax.div(lane, rows) - 1) * side
    slot = block * tiles + lax.div(lax.rem(lane, rows), TILE) - t + REACH
    diagonal = lax.broadcasted_iota(jnp.int32, (heads, heads), 0) == lax.broadcasted_iota(
        jnp.int32, (heads, heads), 1
    )
    rank = jnp.zeros((heads, 3 * rows), F32)
    for s in range(slots):
        row = jnp.broadcast_to(offsets_t[s : s + 1, :], (heads, heads)).astype(F32)
        own = jnp.sum(jnp.where(diagonal, row, 0.0), axis=1, keepdims=True)
        rank = rank + jnp.where(own == slot.astype(F32), float(s), 0.0)
    here = position * tiles + t
    tile = lax.broadcasted_iota(jnp.int32, (heads, ntiles), 1)
    used = jnp.sum(jnp.where(tile == here, counts_t.astype(F32), 0.0), axis=1, keepdims=True)
    key = here + slot - REACH
    inside = (slot >= 0) & (slot < slots) & (key >= 0) & (key < ntiles)
    return jnp.where(inside & ((slot == REACH) | (rank < used)), 1.0, 0.0)


def masked_terms(scores, scale, mask_ref, h, first):
    rows, wide = scores.shape
    mask = jnp.concatenate(
        [
            jnp.broadcast_to(mask_ref[t, h : h + 1, first : first + wide], (TILE, wide))
            for t in range(rows // TILE)
        ],
        axis=0,
    )
    return jnp.exp2(scores * (scale * math.log2(math.e))) * mask


def normal(raw, gain):
    rows = raw.astype(F32)
    return (rows * inverse_spread(rows, 1) * gain).astype(BF16)


def prepare_kernel(
    q_ref, k_ref, v_ref, g_ref, offsets_ref, counts_ref, qgain_ref, kgain_ref,
    qn_ref, qt_ref, gt_ref, kn_ref, kt_ref, unit_ref, inverse_ref, own_ref, mask_ref,
):
    width = qgain_ref.shape[1]
    rows = q_ref.shape[0]
    scale = width ** (-0.5)
    q_gain = qgain_ref[...]
    k_gain = kgain_ref[...]
    position = lax.axis_index("seq")
    for t in range(rows // TILE):
        mask_ref[t] = window_mask(offsets_ref[...], counts_ref[...], position, t, rows)
    for h, cols in enumerate(head_columns(q_ref, width)):
        q = q_ref[:, cols].astype(F32)
        inverse = inverse_spread(q, 1)
        unit = q * inverse
        unit_ref[:, cols] = unit
        inverse_ref[:, cols] = jnp.broadcast_to(inverse, (rows, width))
        qn = (unit * q_gain).astype(BF16)
        qn_ref[:, cols] = qn
        qt_ref[cols, :] = qn.T
        grads = g_ref[:, cols]
        gt_ref[cols, :] = grads.T
        raw = k_ref[:, cols]
        kt_ref[cols, :] = raw.T
        kn = normal(raw, k_gain)
        kn_ref[:, cols] = kn
        own_ref[0, :, cols] = masked_terms(dot(qn, kn, NT), scale, mask_ref, h, rows)
        own_ref[1, :, cols] = dot(grads, v_ref[:, cols], NT)


def attend_kernel(
    qn_ref, g_ref, qt_ref, gt_ref, kn_ref, v_ref, nk_ref, nv_ref, fk_ref, fv_ref,
    mask_ref, unit_ref, inverse_ref, terms_ref, qgain_ref, kgain_ref,
    out_hbm, qgrad_hbm, own_hbm, far_hbm, near_hbm, sum_ref,
    out_ref, qgrad_ref, own_ref, to_far_ref, to_near_ref, sems,
):
    width = qgain_ref.shape[1]
    rows = qn_ref.shape[0]
    scale = width ** (-0.5)
    q_gain = qgain_ref[...]
    k_gain = kgain_ref[...]
    heads = head_columns(qn_ref, width)
    count = len(heads)
    copies = []

    def first_stage(h):
        cols = heads[h]
        k_far, k_near = normal(fk_ref[:, cols], k_gain), normal(nk_ref[:, cols], k_gain)
        v_far, v_near = fv_ref[:, cols], nv_ref[:, cols]
        keys = jnp.concatenate([k_far, kn_ref[:, cols], k_near], axis=0)
        scores = dot(qn_ref[:, cols], jnp.concatenate([k_far, k_near], axis=0), NT)
        dprob = dot(g_ref[:, cols], jnp.concatenate([v_far, v_near], axis=0), NT)
        return keys, scores, dprob

    def middle_stage(h, keys, scores, dprob):
        cols = heads[h]
        terms = [
            masked_terms(scores[:, :rows], scale, mask_ref, h, 0),
            terms_ref[0, :, cols],
            masked_terms(scores[:, rows:], scale, mask_ref, h, 2 * rows),
        ]
        inverse = 1.0 / jnp.sum(terms[0] + terms[1] + terms[2], axis=1, keepdims=True)
        probs = [term * inverse for term in terms]
        dprobs = [dprob[:, :rows], terms_ref[1, :, cols], dprob[:, rows:]]
        delta = jnp.sum(
            probs[0] * dprobs[0] + probs[1] * dprobs[1] + probs[2] * dprobs[2], axis=1, keepdims=True
        )
        dscore = [(p * (d - delta)).astype(BF16) for p, d in zip(probs, dprobs)]
        weights = [p.astype(BF16) for p in probs]
        return keys, jnp.concatenate(dscore, axis=1), jnp.concatenate(weights, axis=1)

    def last_stage(h, keys, dscore, weights, total_gain):
        cols = heads[h]
        vals = jnp.concatenate([fv_ref[:, cols], v_ref[:, cols], nv_ref[:, cols]], axis=0)
        grad_qn = dot(dscore, keys, NN) * scale
        out_ref[:, cols] = dot(weights, vals, NN).astype(BF16)
        key_t = dot(qt_ref[cols, :], dscore, NN) * scale
        val_t = dot(gt_ref[cols, :], weights, NN)
        own_ref[0, cols, :] = key_t[:, rows : 2 * rows]
        own_ref[1, cols, :] = val_t[:, rows : 2 * rows]
        to_far_ref[0, cols, :] = key_t[:, :rows].astype(BF16)
        to_far_ref[1, cols, :] = val_t[:, :rows].astype(BF16)
        to_near_ref[0, cols, :] = key_t[:, 2 * rows :].astype(BF16)
        to_near_ref[1, cols, :] = val_t[:, 2 * rows :].astype(BF16)
        unit = unit_ref[:, cols]
        product = grad_qn * unit
        mean = jnp.mean(product * q_gain, axis=1, keepdims=True)
        qgrad_ref[:, cols] = ((grad_qn * q_gain - unit * mean) * inverse_ref[:, cols]).astype(BF16)
        if h % GROUP == GROUP - 1:
            i = h // GROUP
            span = slice(heads[h - GROUP + 1].start, cols.stop)
            pairs = [
                (to_far_ref.at[:, span, :], far_hbm.at[:, span, :]),
                (to_near_ref.at[:, span, :], near_hbm.at[:, span, :]),
                (own_ref.at[:, span, :], own_hbm.at[:, span, :]),
                (out_ref.at[:, span], out_hbm.at[:, span]),
                (qgrad_ref.at[:, span], qgrad_hbm.at[:, span]),
            ]
            for j, (here, there) in enumerate(pairs):
                copy = pltpu.make_async_copy(here, there, sems.at[i, j])
                copy.start()
                copies.append(copy)
        return total_gain + product

    total_gain = jnp.zeros((rows, width), F32)
    ahead = first_stage(0)
    behind = None
    for h in range(count):
        now = ahead
        if h + 1 < count:
            ahead = first_stage(h + 1)
        now = middle_stage(h, *now)
        if behind is not None:
            total_gain = last_stage(h - 1, *behind, total_gain)
        behind = now
    total_gain = last_stage(count - 1, *behind, total_gain)
    sum_ref[...] = jnp.sum(total_gain, axis=0, keepdims=True)
    for copy in copies:
        copy.wait()


def finish_kernel(kt_ref, own_ref, far_ref, near_ref, gain_ref, kgrad_ref, vgrad_ref, inverse_ref):
    width = gain_ref.shape[1]
    row = gain_ref[...]
    inverse_ref[...] = 1.0 / row
    diagonal = lax.broadcasted_iota(jnp.int32, (width, width), 0) == lax.broadcasted_iota(
        jnp.int32, (width, width), 1
    )
    gain = jnp.sum(jnp.where(diagonal, jnp.broadcast_to(row, (width, width)), 0.0), axis=1, keepdims=True)
    for cols in head_columns(kgrad_ref, width):

        def total(i):
            return own_ref[i, cols, :] + far_ref[i, cols, :].astype(F32) + near_ref[i, cols, :].astype(F32)

        k = kt_ref[cols, :].astype(F32)
        inverse = inverse_spread(k, 0)
        unit = k * inverse
        scaled = total(0) * gain
        mean = jnp.mean(scaled * unit, axis=0, keepdims=True)
        kgrad_ref[:, cols] = ((scaled - unit * mean) * inverse).astype(BF16).T
        vgrad_ref[:, cols] = total(1).astype(BF16).T


def gain_kernel(parts_ref, q_ref, inverse_ref, qgain_ref, kgain_ref):
    total = jnp.sum(parts_ref[...], axis=0)
    qgain_ref[...] = total
    kgain_ref[...] = total * q_ref[...] * inverse_ref[...]


def call(body, out_shape, flops, in_specs=None, out_specs=None, scratch=(), grid=(), vmem=24):
    whole = pl.BlockSpec(memory_space=pltpu.VMEM)

    def run(*args):
        return pl.pallas_call(
            body,
            grid=grid,
            in_specs=in_specs or [whole] * len(args),
            out_specs=out_specs or [whole] * len(out_shape),
            out_shape=out_shape,
            scratch_shapes=scratch,
            compiler_params=pltpu.CompilerParams(vmem_limit_bytes=vmem * 1024 * 1024),
            cost_estimate=pl.CostEstimate(flops=flops, bytes_accessed=4 << 20, transcendentals=0),
        )(*args)

    return run


def spread_over(axis, vector):
    size = lax.axis_size(axis)
    return lax.all_to_all(jnp.broadcast_to(vector[None], (size,) + vector.shape), axis, 0, 0)


def shards(q_raw, k_raw, values, d_out, q_gain, k_gain, offsets, counts):
    rows, columns = q_raw.shape[1:]
    width = q_gain.shape[0]
    heads = offsets.shape[0]
    q, k, v, g = q_raw[0], k_raw[0], values[0], d_out[0]
    q_row, k_row = q_gain[None], k_gain[None]

    def like(*shape, dtype=BF16):
        return jax.ShapeDtypeStruct(shape, dtype)

    hbm = pl.BlockSpec(memory_space=pltpu.HBM)
    vmem = pl.BlockSpec(memory_space=pltpu.VMEM)
    products = 2 * rows * rows * columns
    flat = like(rows, columns)
    turned = like(columns, rows)
    part = like(2, columns, rows)
    own_part = like(2, columns, rows, dtype=F32)

    far_k, far_v = swap(k, 1), swap(v, 1)
    near_k, near_v = swap(k, 0), swap(v, 0)
    wide = like(rows, columns, dtype=F32)
    qn, qt, gt, kn, kt, unit, inverse, terms, mask = call(
        prepare_kernel,
        [flat, turned, turned, flat, turned, wide, wide, like(2, rows, columns, dtype=F32)]
        + [like(rows // TILE, heads, 3 * rows, dtype=F32)],
        2 * products,
    )(q, k, v, g, offsets.T, counts.T, q_row, k_row)
    out, q_grad, own, to_far, to_near, gain = call(
        attend_kernel,
        [flat, flat, own_part, part, part, like(1, width, dtype=F32)],
        16 * products,
        out_specs=[hbm] * 5 + [vmem],
        scratch=[
            pltpu.VMEM((rows, columns), BF16),
            pltpu.VMEM((rows, columns), BF16),
            pltpu.VMEM((2, columns, rows), F32),
            pltpu.VMEM((2, columns, rows), BF16),
            pltpu.VMEM((2, columns, rows), BF16),
            pltpu.SemaphoreType.DMA((heads // GROUP, 5)),
        ],
    )(qn, g, qt, gt, kn, v, near_k, near_v, far_k, far_v, mask, unit, inverse, terms, q_row, k_row)
    from_far = swap(to_far, 1)
    from_near = swap(to_near, 0)
    chunk = STEP * width
    flat_spec = pl.BlockSpec((rows, chunk), lambda j: (0, j))
    turned_spec = pl.BlockSpec((chunk, rows), lambda j: (j, 0))
    part_spec = pl.BlockSpec((2, chunk, rows), lambda j: (0, j, 0))
    row_spec = pl.BlockSpec((1, width), lambda j: (0, 0))
    k_grad, v_grad, inverse_gain = call(
        finish_kernel,
        [flat, flat, like(1, width, dtype=F32)],
        rows * columns * 40,
        in_specs=[turned_spec, part_spec, part_spec, part_spec, row_spec],
        out_specs=[flat_spec, flat_spec, row_spec],
        grid=(heads // STEP,),
    )(kt, own, from_far, from_near, k_row)
    parts = spread_over("seq", jnp.sum(spread_over("dp", gain), axis=0))
    gains = [like(1, width, dtype=F32)] * 2
    q_gain_grad, k_gain_grad = call(gain_kernel, gains, 0)(parts, q_row, inverse_gain)
    return (
        out[None],
        q_grad[None],
        k_grad[None],
        v_grad[None],
        q_gain_grad[0],
        k_gain_grad[0],
    )


def solution(mesh):
    tokens = P("dp", "seq", None)
    return jax.shard_map(
        shards,
        mesh=mesh,
        in_specs=(tokens, tokens, tokens, tokens, P(), P(), P(), P()),
        out_specs=(tokens, tokens, tokens, tokens, P(), P()),
        check_vma=False,
    )
```

```python
import math

import jax
import jax.numpy as jnp
from jax import lax
from jax.experimental import pallas as pl
from jax.experimental.pallas import tpu as pltpu
from jax.sharding import PartitionSpec as P

TILE = 64
REACH = 2
EPS = 1e-06
GROUP = 6
STEP = 3
IDLE = 5 * 10**9
COMBINE = 30 * 10**9
NT = (((1,), (1,)), ((), ()))
NN = (((1,), (0,)), ((), ()))
F32 = jnp.float32
BF16 = jnp.bfloat16


def dot(a, b, dims):
    return lax.dot_general(a, b, dims, preferred_element_type=F32)


def inverse_spread(rows, axis):
    return lax.rsqrt(jnp.mean(rows * rows, axis=axis, keepdims=True) + EPS)


def swap(block, parity):
    size = lax.axis_size("seq")
    route = [(i, i + 1 if i % 2 == parity else i - 1) for i in range(size)]
    return lax.ppermute(block, "seq", [(i, j) for i, j in route if 0 <= j < size])


def head_columns(ref, width):
    return [slice(h * width, (h + 1) * width) for h in range(ref.shape[-1] // width)]


def window_mask(offsets_t, counts_t, identity, position, t, rows):
    slots, heads = offsets_t.shape
    ntiles = counts_t.shape[1]
    tiles = rows // TILE
    lane = lax.broadcasted_iota(jnp.int32, (heads, 3 * rows), 1)
    side = 1 - 2 * lax.rem(position, 2)
    block = (lax.div(lane, rows) - 1) * side
    slot = block * tiles + lax.div(lax.rem(lane, rows), TILE) - t + REACH
    rank = jnp.zeros((heads, 3 * rows), F32)
    for s in range(slots):
        row = jnp.broadcast_to(offsets_t[s : s + 1, :], (heads, heads)).astype(F32)
        own = jnp.sum(row * identity, axis=1, keepdims=True)
        rank = rank + jnp.where(own == slot.astype(F32), float(s), 0.0)
    here = position * tiles + t
    tile = lax.broadcasted_iota(jnp.int32, (heads, ntiles), 1)
    used = jnp.sum(jnp.where(tile == here, counts_t.astype(F32), 0.0), axis=1, keepdims=True)
    key = here + slot - REACH
    inside = (slot >= 0) & (slot < slots) & (key >= 0) & (key < ntiles)
    return jnp.where(inside & ((slot == REACH) | (rank < used)), 1.0, 0.0)


def masked_terms(scores, scale, mask_ref, h, first):
    rows, wide = scores.shape
    mask = jnp.concatenate(
        [
            jnp.broadcast_to(mask_ref[t, h : h + 1, first : first + wide], (TILE, wide))
            for t in range(rows // TILE)
        ],
        axis=0,
    )
    return jnp.exp2(scores * (scale * math.log2(math.e))) * mask


def normal(raw, gain):
    rows = raw.astype(F32)
    return (rows * inverse_spread(rows, 1) * gain).astype(BF16)


def identity_kernel(identity_ref):
    size = identity_ref.shape[0]
    line = lax.broadcasted_iota(jnp.int32, (size, size), 0)
    identity_ref[...] = jnp.where(line == lax.broadcasted_iota(jnp.int32, (size, size), 1), 1.0, 0.0)


def prepare_kernel(
    q_ref, k_ref, v_ref, g_ref, offsets_ref, counts_ref, identity_ref, qgain_ref, kgain_ref,
    qn_ref, qt_ref, gt_ref, kv_ref, kt_ref, unit_ref, inverse_ref, own_ref, mask_ref,
):
    width = qgain_ref.shape[1]
    rows = q_ref.shape[0]
    scale = width ** (-0.5)
    q_gain = qgain_ref[...]
    k_gain = kgain_ref[...]
    position = lax.axis_index("seq")
    heads = offsets_ref.shape[1]
    identity = identity_ref[:heads, :heads]
    for t in range(rows // TILE):
        mask_ref[t] = window_mask(offsets_ref[...], counts_ref[...], identity, position, t, rows)
    for h, cols in enumerate(head_columns(q_ref, width)):
        q = q_ref[:, cols].astype(F32)
        inverse = inverse_spread(q, 1)
        unit = q * inverse
        unit_ref[:, cols] = unit
        inverse_ref[:, cols] = jnp.broadcast_to(inverse, (rows, width))
        qn = (unit * q_gain).astype(BF16)
        qn_ref[:, cols] = qn
        qt_ref[cols, :] = qn.T
        grads = g_ref[:, cols]
        gt_ref[cols, :] = grads.T
        raw = k_ref[:, cols]
        kt_ref[cols, :] = raw.T
        kn = normal(raw, k_gain)
        vals = v_ref[:, cols]
        kv_ref[0, :, cols] = kn
        kv_ref[1, :, cols] = vals
        own_ref[0, :, cols] = masked_terms(dot(qn, kn, NT), scale, mask_ref, h, rows)
        own_ref[1, :, cols] = dot(grads, vals, NT)


def far_kernel(k_ref, gain_ref, kn_ref):
    gain = gain_ref[...]
    for cols in head_columns(k_ref, gain_ref.shape[1]):
        kn_ref[:, cols] = normal(k_ref[:, cols], gain)


def attend_kernel(
    qn_ref, g_ref, qt_ref, gt_ref, kv_ref, near_ref, fk_ref, fv_ref,
    mask_ref, unit_ref, inverse_ref, terms_ref, qgain_ref,
    out_hbm, qgrad_hbm, own_hbm, far_hbm, near_hbm, sum_ref,
    out_ref, qgrad_ref, own_ref, to_far_ref, to_near_ref, sems,
):
    width = qgain_ref.shape[1]
    rows = qn_ref.shape[0]
    scale = width ** (-0.5)
    q_gain = qgain_ref[...]
    heads = head_columns(qn_ref, width)
    count = len(heads)
    copies = []

    def first_stage(h):
        cols = heads[h]
        k_far, k_near = fk_ref[:, cols], near_ref[0, :, cols]
        v_far, v_near = fv_ref[:, cols], near_ref[1, :, cols]
        keys = jnp.concatenate([k_far, kv_ref[0, :, cols], k_near], axis=0)
        scores = dot(qn_ref[:, cols], jnp.concatenate([k_far, k_near], axis=0), NT)
        dprob = dot(g_ref[:, cols], jnp.concatenate([v_far, v_near], axis=0), NT)
        return keys, scores, dprob

    def middle_stage(h, keys, scores, dprob):
        cols = heads[h]
        terms = [
            masked_terms(scores[:, :rows], scale, mask_ref, h, 0),
            terms_ref[0, :, cols],
            masked_terms(scores[:, rows:], scale, mask_ref, h, 2 * rows),
        ]
        inverse = 1.0 / jnp.sum(terms[0] + terms[1] + terms[2], axis=1, keepdims=True)
        probs = [term * inverse for term in terms]
        dprobs = [dprob[:, :rows], terms_ref[1, :, cols], dprob[:, rows:]]
        delta = jnp.sum(
            probs[0] * dprobs[0] + probs[1] * dprobs[1] + probs[2] * dprobs[2], axis=1, keepdims=True
        )
        dscore = [(p * (d - delta)).astype(BF16) for p, d in zip(probs, dprobs)]
        weights = [p.astype(BF16) for p in probs]
        return keys, jnp.concatenate(dscore, axis=1), jnp.concatenate(weights, axis=1)

    def last_stage(h, keys, dscore, weights, total_gain):
        cols = heads[h]
        vals = jnp.concatenate([fv_ref[:, cols], kv_ref[1, :, cols], near_ref[1, :, cols]], axis=0)
        grad_qn = dot(dscore, keys, NN) * scale
        out_ref[:, cols] = dot(weights, vals, NN).astype(BF16)
        key_t = dot(qt_ref[cols, :], dscore, NN) * scale
        val_t = dot(gt_ref[cols, :], weights, NN)
        own_ref[0, cols, :] = key_t[:, rows : 2 * rows]
        own_ref[1, cols, :] = val_t[:, rows : 2 * rows]
        to_far_ref[0, cols, :] = key_t[:, :rows].astype(BF16)
        to_far_ref[1, cols, :] = val_t[:, :rows].astype(BF16)
        to_near_ref[0, cols, :] = key_t[:, 2 * rows :].astype(BF16)
        to_near_ref[1, cols, :] = val_t[:, 2 * rows :].astype(BF16)
        unit = unit_ref[:, cols]
        product = grad_qn * unit
        mean = jnp.mean(product * q_gain, axis=1, keepdims=True)
        qgrad_ref[:, cols] = ((grad_qn * q_gain - unit * mean) * inverse_ref[:, cols]).astype(BF16)
        if h % GROUP == GROUP - 1:
            i = h // GROUP
            span = slice(heads[h - GROUP + 1].start, cols.stop)
            pairs = [
                (to_far_ref.at[:, span, :], far_hbm.at[:, span, :]),
                (to_near_ref.at[:, span, :], near_hbm.at[:, span, :]),
                (own_ref.at[:, span, :], own_hbm.at[:, span, :]),
                (out_ref.at[:, span], out_hbm.at[:, span]),
                (qgrad_ref.at[:, span], qgrad_hbm.at[:, span]),
            ]
            for j, (here, there) in enumerate(pairs):
                copy = pltpu.make_async_copy(here, there, sems.at[i, j])
                copy.start()
                copies.append(copy)
        return total_gain + product

    total_gain = jnp.zeros((rows, width), F32)
    ahead = first_stage(0)
    behind = None
    for h in range(count):
        now = ahead
        if h + 1 < count:
            ahead = first_stage(h + 1)
        now = middle_stage(h, *now)
        if behind is not None:
            total_gain = last_stage(h - 1, *behind, total_gain)
        behind = now
    total_gain = last_stage(count - 1, *behind, total_gain)
    sum_ref[...] = jnp.sum(total_gain, axis=0, keepdims=True)
    for copy in copies:
        copy.wait()


def finish_kernel(kt_ref, own_ref, far_ref, near_ref, identity_ref, gain_ref, kgrad_ref, vgrad_ref, inverse_ref):
    width = gain_ref.shape[1]
    row = gain_ref[...]
    inverse_ref[...] = 1.0 / row
    gain = jnp.sum(row * identity_ref[...], axis=1, keepdims=True)
    for cols in head_columns(kgrad_ref, width):

        def total(i):
            return own_ref[i, cols, :] + far_ref[i, cols, :].astype(F32) + near_ref[i, cols, :].astype(F32)

        k = kt_ref[cols, :].astype(F32)
        inverse = inverse_spread(k, 0)
        unit = k * inverse
        scaled = total(0) * gain
        mean = jnp.mean(scaled * unit, axis=0, keepdims=True)
        kgrad_ref[:, cols] = ((scaled - unit * mean) * inverse).astype(BF16).T
        vgrad_ref[:, cols] = total(1).astype(BF16).T


def combine_kernel(parts_ref, spread_ref):
    spread_ref[...] = jnp.broadcast_to(jnp.sum(parts_ref[...], axis=0, keepdims=True), spread_ref.shape)


def gain_kernel(parts_ref, q_ref, inverse_ref, qgain_ref, kgain_ref):
    total = jnp.sum(parts_ref[...], axis=0)
    qgain_ref[...] = total
    kgain_ref[...] = total * q_ref[...] * inverse_ref[...]


def call(body, out_shape, flops, in_specs=None, out_specs=None, scratch=(), grid=(), vmem=24):
    whole = pl.BlockSpec(memory_space=pltpu.VMEM)

    def run(*args):
        return pl.pallas_call(
            body,
            grid=grid,
            in_specs=in_specs or [whole] * len(args),
            out_specs=out_specs or [whole] * len(out_shape),
            out_shape=out_shape,
            scratch_shapes=scratch,
            compiler_params=pltpu.CompilerParams(vmem_limit_bytes=vmem * 1024 * 1024),
            cost_estimate=pl.CostEstimate(flops=flops, bytes_accessed=4 << 20, transcendentals=0),
        )(*args)

    return run


def over(axis, vector):
    return jnp.broadcast_to(vector[None], (lax.axis_size(axis),) + vector.shape)


def exchange(parts, axis):
    return lax.all_to_all(parts, axis, 0, 0)


def shards(q_raw, k_raw, values, d_out, q_gain, k_gain, offsets, counts):
    rows, columns = q_raw.shape[1:]
    width = q_gain.shape[0]
    heads = offsets.shape[0]
    q, k, v, g = q_raw[0], k_raw[0], values[0], d_out[0]
    q_row, k_row = q_gain[None], k_gain[None]

    def like(*shape, dtype=BF16):
        return jax.ShapeDtypeStruct(shape, dtype)

    hbm = pl.BlockSpec(memory_space=pltpu.HBM)
    vmem = pl.BlockSpec(memory_space=pltpu.VMEM)
    products = 2 * rows * rows * columns
    flat = like(rows, columns)
    turned = like(columns, rows)
    part = like(2, columns, rows)
    own_part = like(2, columns, rows, dtype=F32)

    far_k, far_v = swap(k, 1), swap(v, 1)
    (identity,) = call(identity_kernel, [like(width, width, dtype=F32)], IDLE)()
    wide = like(rows, columns, dtype=F32)
    qn, qt, gt, kv, kt, unit, inverse, terms, mask = call(
        prepare_kernel,
        [flat, turned, turned, like(2, rows, columns), turned, wide, wide]
        + [like(2, rows, columns, dtype=F32), like(rows // TILE, heads, 3 * rows, dtype=F32)],
        2 * products,
    )(q, k, v, g, offsets.T, counts.T, identity, q_row, k_row)
    near = swap(kv, 0)
    (far_k,) = call(far_kernel, [flat], 2 * IDLE)(far_k, k_row)
    out, q_grad, own, to_far, to_near, gain = call(
        attend_kernel,
        [flat, flat, own_part, part, part, like(1, width, dtype=F32)],
        16 * products,
        out_specs=[hbm] * 5 + [vmem],
        scratch=[
            pltpu.VMEM((rows, columns), BF16),
            pltpu.VMEM((rows, columns), BF16),
            pltpu.VMEM((2, columns, rows), F32),
            pltpu.VMEM((2, columns, rows), BF16),
            pltpu.VMEM((2, columns, rows), BF16),
            pltpu.SemaphoreType.DMA((heads // GROUP, 5)),
        ],
    )(qn, g, qt, gt, kv, near, far_k, far_v, mask, unit, inverse, terms, q_row)
    from_far = swap(to_far, 1)
    from_near = swap(to_near, 0)
    chunk = STEP * width
    flat_spec = pl.BlockSpec((rows, chunk), lambda j: (0, j))
    turned_spec = pl.BlockSpec((chunk, rows), lambda j: (j, 0))
    part_spec = pl.BlockSpec((2, chunk, rows), lambda j: (0, j, 0))
    row_spec = pl.BlockSpec((1, width), lambda j: (0, 0))
    square_spec = pl.BlockSpec((width, width), lambda j: (0, 0))
    k_grad, v_grad, inverse_gain = call(
        finish_kernel,
        [flat, flat, like(1, width, dtype=F32)],
        rows * columns * 40,
        in_specs=[turned_spec, part_spec, part_spec, part_spec, square_spec, row_spec],
        out_specs=[flat_spec, flat_spec, row_spec],
        grid=(heads // STEP,),
    )(kt, own, from_far, from_near, identity, k_row)
    spread = [like(lax.axis_size("seq"), 1, width, dtype=F32)]
    (spread,) = call(combine_kernel, spread, COMBINE)(exchange(over("dp", gain), "dp"))
    parts = exchange(spread, "seq")
    gains = [like(1, width, dtype=F32)] * 2
    q_gain_grad, k_gain_grad = call(gain_kernel, gains, 0)(parts, q_row, inverse_gain)
    return (
        out[None],
        q_grad[None],
        k_grad[None],
        v_grad[None],
        q_gain_grad[0],
        k_gain_grad[0],
    )


def solution(mesh):
    tokens = P("dp", "seq", None)
    return jax.shard_map(
        shards,
        mesh=mesh,
        in_specs=(tokens, tokens, tokens, tokens, P(), P(), P(), P()),
        out_specs=(tokens, tokens, tokens, tokens, P(), P()),
        check_vma=False,
    )
```

```python
import math

import jax
import jax.numpy as jnp
from jax import lax
from jax.experimental import pallas as pl
from jax.experimental.pallas import tpu as pltpu
from jax.sharding import PartitionSpec as P

TILE = 64
REACH = 2
EPS = 1e-06
GROUP = 6
STEP = 6
IDLE = 5 * 10**9
COMBINE = 30 * 10**9
NT = (((1,), (1,)), ((), ()))
NN = (((1,), (0,)), ((), ()))
F32 = jnp.float32
BF16 = jnp.bfloat16


def dot(a, b, dims):
    return lax.dot_general(a, b, dims, preferred_element_type=F32)


def inverse_spread(rows, axis):
    return lax.rsqrt(jnp.mean(rows * rows, axis=axis, keepdims=True) + EPS)


def swap(block, parity):
    size = lax.axis_size("seq")
    route = [(i, i + 1 if i % 2 == parity else i - 1) for i in range(size)]
    return lax.ppermute(block, "seq", [(i, j) for i, j in route if 0 <= j < size])


def head_columns(ref, width):
    return [slice(h * width, (h + 1) * width) for h in range(ref.shape[-1] // width)]


def window_mask(offsets_t, counts_t, identity, position, t, rows):
    slots, heads = offsets_t.shape
    ntiles = counts_t.shape[1]
    tiles = rows // TILE
    lane = lax.broadcasted_iota(jnp.int32, (heads, 3 * rows), 1)
    side = 1 - 2 * lax.rem(position, 2)
    block = (lax.div(lane, rows) - 1) * side
    slot = block * tiles + lax.div(lax.rem(lane, rows), TILE) - t + REACH
    rank = jnp.zeros((heads, 3 * rows), F32)
    for s in range(slots):
        row = jnp.broadcast_to(offsets_t[s : s + 1, :], (heads, heads)).astype(F32)
        own = jnp.sum(row * identity, axis=1, keepdims=True)
        rank = rank + jnp.where(own == slot.astype(F32), float(s), 0.0)
    here = position * tiles + t
    tile = lax.broadcasted_iota(jnp.int32, (heads, ntiles), 1)
    used = jnp.sum(jnp.where(tile == here, counts_t.astype(F32), 0.0), axis=1, keepdims=True)
    key = here + slot - REACH
    inside = (slot >= 0) & (slot < slots) & (key >= 0) & (key < ntiles)
    return jnp.where(inside & ((slot == REACH) | (rank < used)), 1.0, 0.0)


def masked_terms(scores, scale, mask_ref, h, first):
    rows, wide = scores.shape
    mask = jnp.concatenate(
        [
            jnp.broadcast_to(mask_ref[t, h : h + 1, first : first + wide], (TILE, wide))
            for t in range(rows // TILE)
        ],
        axis=0,
    )
    return jnp.exp2(scores * (scale * math.log2(math.e))) * mask


def normal(raw, gain):
    rows = raw.astype(F32)
    return (rows * inverse_spread(rows, 1) * gain).astype(BF16)


def identity_kernel(identity_ref):
    size = identity_ref.shape[0]
    line = lax.broadcasted_iota(jnp.int32, (size, size), 0)
    identity_ref[...] = jnp.where(line == lax.broadcasted_iota(jnp.int32, (size, size), 1), 1.0, 0.0)


def prepare_kernel(
    q_ref, k_ref, v_ref, g_ref, offsets_ref, counts_ref, identity_ref, qgain_ref, kgain_ref,
    qn_ref, qt_ref, gt_ref, kv_ref, kt_ref, unit_ref, inverse_ref, own_ref, mask_ref,
):
    width = qgain_ref.shape[1]
    rows = q_ref.shape[0]
    scale = width ** (-0.5)
    q_gain = qgain_ref[...]
    k_gain = kgain_ref[...]
    position = lax.axis_index("seq")
    heads = offsets_ref.shape[1]
    identity = identity_ref[:heads, :heads]
    for t in range(rows // TILE):
        mask_ref[t] = window_mask(offsets_ref[...], counts_ref[...], identity, position, t, rows)
    for h, cols in enumerate(head_columns(q_ref, width)):
        q = q_ref[:, cols].astype(F32)
        inverse = inverse_spread(q, 1)
        unit = q * inverse
        unit_ref[:, cols] = unit
        inverse_ref[:, cols] = jnp.broadcast_to(inverse, (rows, width))
        qn = (unit * q_gain).astype(BF16)
        qn_ref[:, cols] = qn
        qt_ref[cols, :] = qn.T
        grads = g_ref[:, cols]
        gt_ref[cols, :] = grads.T
        raw = k_ref[:, cols]
        kt_ref[cols, :] = raw.T
        kn = normal(raw, k_gain)
        vals = v_ref[:, cols]
        kv_ref[0, :, cols] = kn
        kv_ref[1, :, cols] = vals
        own_ref[0, :, cols] = masked_terms(dot(qn, kn, NT), scale, mask_ref, h, rows)
        own_ref[1, :, cols] = dot(grads, vals, NT)


def far_kernel(k_ref, gain_ref, kn_ref):
    gain = gain_ref[...]
    for cols in head_columns(k_ref, gain_ref.shape[1]):
        kn_ref[:, cols] = normal(k_ref[:, cols], gain)


def side_kernel(qn_ref, g_ref, near_ref, fk_ref, mask_ref, gain_ref, terms_ref):
    width = gain_ref.shape[1]
    rows = qn_ref.shape[0]
    scale = width ** (-0.5)
    for h, cols in enumerate(head_columns(qn_ref, width)):
        scores = dot(qn_ref[:, cols], jnp.concatenate([fk_ref[:, cols], near_ref[0, :, cols]], axis=0), NT)
        terms_ref[0, :, cols] = masked_terms(scores[:, :rows], scale, mask_ref, h, 0)
        terms_ref[1, :, cols] = masked_terms(scores[:, rows:], scale, mask_ref, h, 2 * rows)
        terms_ref[2, :, cols] = dot(g_ref[:, cols], near_ref[1, :, cols], NT)


def attend_kernel(
    qn_ref, g_ref, qt_ref, gt_ref, kv_ref, near_ref, fk_ref, fv_ref,
    side_ref, unit_ref, inverse_ref, terms_ref, qgain_ref,
    out_hbm, qgrad_hbm, own_ref, far_hbm, near_hbm, spread_hbm,
    out_ref, qgrad_ref, to_far_ref, to_near_ref, spread_ref, sems,
):
    width = qgain_ref.shape[1]
    rows = qn_ref.shape[0]
    scale = width ** (-0.5)
    q_gain = qgain_ref[...]
    heads = head_columns(qn_ref, width)
    count = len(heads)
    copies = []

    def first_stage(h):
        return (dot(g_ref[:, heads[h]], fv_ref[:, heads[h]], NT),)

    def middle_stage(h, dprob):
        cols = heads[h]
        terms = [side_ref[0, :, cols], terms_ref[0, :, cols], side_ref[1, :, cols]]
        inverse = 1.0 / jnp.sum(terms[0] + terms[1] + terms[2], axis=1, keepdims=True)
        probs = [term * inverse for term in terms]
        dprobs = [dprob, terms_ref[1, :, cols], side_ref[2, :, cols]]
        delta = jnp.sum(
            probs[0] * dprobs[0] + probs[1] * dprobs[1] + probs[2] * dprobs[2], axis=1, keepdims=True
        )
        dscore = [(p * (d - delta)).astype(BF16) for p, d in zip(probs, dprobs)]
        weights = [p.astype(BF16) for p in probs]
        return jnp.concatenate(dscore, axis=1), jnp.concatenate(weights, axis=1)

    def last_stage(h, dscore, weights, total_gain):
        cols = heads[h]
        keys = jnp.concatenate([fk_ref[:, cols], kv_ref[0, :, cols], near_ref[0, :, cols]], axis=0)
        vals = jnp.concatenate([fv_ref[:, cols], kv_ref[1, :, cols], near_ref[1, :, cols]], axis=0)
        grad_qn = dot(dscore, keys, NN) * scale
        out_ref[:, cols] = dot(weights, vals, NN).astype(BF16)
        key_t = dot(qt_ref[cols, :], dscore, NN) * scale
        val_t = dot(gt_ref[cols, :], weights, NN)
        own_ref[0, cols, :] = key_t[:, rows : 2 * rows].astype(BF16)
        own_ref[1, cols, :] = val_t[:, rows : 2 * rows].astype(BF16)
        to_far_ref[0, cols, :] = key_t[:, :rows].astype(BF16)
        to_far_ref[1, cols, :] = val_t[:, :rows].astype(BF16)
        to_near_ref[0, cols, :] = key_t[:, 2 * rows :].astype(BF16)
        to_near_ref[1, cols, :] = val_t[:, 2 * rows :].astype(BF16)
        unit = unit_ref[:, cols]
        product = grad_qn * unit
        mean = jnp.mean(product * q_gain, axis=1, keepdims=True)
        qgrad_ref[:, cols] = ((grad_qn * q_gain - unit * mean) * inverse_ref[:, cols]).astype(BF16)
        if h % GROUP == GROUP - 1:
            i = h // GROUP
            span = slice(heads[h - GROUP + 1].start, cols.stop)
            pairs = [
                (to_far_ref.at[:, span, :], far_hbm.at[:, span, :]),
                (to_near_ref.at[:, span, :], near_hbm.at[:, span, :]),
                (out_ref.at[:, span], out_hbm.at[:, span]),
                (qgrad_ref.at[:, span], qgrad_hbm.at[:, span]),
            ]
            for j, (here, there) in enumerate(pairs):
                copy = pltpu.make_async_copy(here, there, sems.at[i, j])
                copy.start()
                copies.append(copy)
        return total_gain + product

    total_gain = jnp.zeros((rows, width), F32)
    ahead = first_stage(0)
    behind = None
    for h in range(count):
        now = ahead
        if h + 1 < count:
            ahead = first_stage(h + 1)
        now = middle_stage(h, *now)
        if behind is not None:
            total_gain = last_stage(h - 1, *behind, total_gain)
        behind = now
    total_gain = last_stage(count - 1, *behind, total_gain)
    sums = jnp.sum(total_gain, axis=0, keepdims=True)
    spread_ref[...] = jnp.broadcast_to(sums[None], spread_ref.shape)
    copies.append(pltpu.make_async_copy(spread_ref, spread_hbm, sems.at[count // GROUP, 0]))
    copies[-1].start()
    for copy in copies:
        copy.wait()


def finish_kernel(
    kt_ref, own_ref, far_ref, near_ref, gain_ref, kgrad_hbm, vgrad_hbm, inverse_ref, kgrad_ref, vgrad_ref, sems
):
    width = gain_ref.shape[1]
    row = gain_ref[...]
    inverse_ref[...] = 1.0 / row
    line = lax.broadcasted_iota(jnp.int32, (width, width), 0)
    diagonal = line == lax.broadcasted_iota(jnp.int32, (width, width), 1)
    gain = jnp.sum(jnp.where(diagonal, jnp.broadcast_to(row, (width, width)), 0.0), axis=1, keepdims=True)
    heads = head_columns(kgrad_ref, width)
    copies = []
    for h, cols in enumerate(heads):

        def total(i):
            return own_ref[i, cols, :].astype(F32) + far_ref[i, cols, :].astype(F32) + near_ref[i, cols, :].astype(F32)

        k = kt_ref[cols, :].astype(F32)
        inverse = inverse_spread(k, 0)
        unit = k * inverse
        scaled = total(0) * gain
        mean = jnp.mean(scaled * unit, axis=0, keepdims=True)
        kgrad_ref[:, cols] = ((scaled - unit * mean) * inverse).astype(BF16).T
        vgrad_ref[:, cols] = total(1).astype(BF16).T
        if h % STEP == STEP - 1:
            i = h // STEP
            span = slice(heads[h - STEP + 1].start, cols.stop)
            for j, (here, there) in enumerate([(kgrad_ref, kgrad_hbm), (vgrad_ref, vgrad_hbm)]):
                copies.append(pltpu.make_async_copy(here.at[:, span], there.at[:, span], sems.at[i, j]))
                copies[-1].start()
    for copy in copies:
        copy.wait()


def combine_kernel(parts_ref, spread_ref):
    spread_ref[...] = jnp.broadcast_to(jnp.sum(parts_ref[...], axis=0, keepdims=True), spread_ref.shape)


def gain_kernel(parts_ref, q_ref, inverse_ref, qgain_ref, kgain_ref):
    total = jnp.sum(parts_ref[...], axis=0)
    qgain_ref[...] = total
    kgain_ref[...] = total * q_ref[...] * inverse_ref[...]


def call(body, out_shape, flops, in_specs=None, out_specs=None, scratch=(), vmem=24):
    whole = pl.BlockSpec(memory_space=pltpu.VMEM)

    def run(*args):
        return pl.pallas_call(
            body,
            in_specs=in_specs or [whole] * len(args),
            out_specs=out_specs or [whole] * len(out_shape),
            out_shape=out_shape,
            scratch_shapes=scratch,
            compiler_params=pltpu.CompilerParams(vmem_limit_bytes=vmem * 1024 * 1024),
            cost_estimate=pl.CostEstimate(flops=flops, bytes_accessed=4 << 20, transcendentals=0),
        )(*args)

    return run


def exchange(parts, axis):
    return lax.all_to_all(parts, axis, 0, 0)


def shards(q_raw, k_raw, values, d_out, q_gain, k_gain, offsets, counts):
    rows, columns = q_raw.shape[1:]
    width = q_gain.shape[0]
    heads = offsets.shape[0]
    q, k, v, g = q_raw[0], k_raw[0], values[0], d_out[0]
    q_row, k_row = q_gain[None], k_gain[None]

    def like(*shape, dtype=BF16):
        return jax.ShapeDtypeStruct(shape, dtype)

    def far_away(shape):
        return pltpu.HBM(shape.shape, shape.dtype)

    hbm = pl.BlockSpec(memory_space=pltpu.HBM)
    vmem = pl.BlockSpec(memory_space=pltpu.VMEM)
    products = 2 * rows * rows * columns
    flat = like(rows, columns)
    turned = like(columns, rows)
    part = like(2, columns, rows)

    far_k, far_v = swap(k, 1), swap(v, 1)
    (identity,) = call(identity_kernel, [like(width, width, dtype=F32)], IDLE)()
    wide = like(rows, columns, dtype=F32)
    qn, qt, gt, kv, kt, unit, inverse, terms, mask = call(
        prepare_kernel,
        [flat, turned, turned, like(2, rows, columns), turned, wide, wide]
        + [like(2, rows, columns, dtype=F32), like(rows // TILE, heads, 3 * rows, dtype=F32)],
        2 * products,
    )(q, k, v, g, offsets.T, counts.T, identity, q_row, k_row)
    near = swap(kv, 0)
    (far_k,) = call(far_kernel, [flat], 2 * IDLE)(far_k, k_row)
    (side,) = call(side_kernel, [like(3, rows, columns, dtype=F32)], 3 * products)(
        qn, g, near, far_k, mask, k_row
    )
    spread_dp = like(lax.axis_size("dp"), 1, width, dtype=F32)
    out, q_grad, own, to_far, to_near, spread = call(
        attend_kernel,
        [far_away(flat), far_away(flat), part, far_away(part), far_away(part), far_away(spread_dp)],
        16 * products,
        out_specs=[hbm, hbm, vmem, hbm, hbm, hbm],
        scratch=[
            pltpu.VMEM((rows, columns), BF16),
            pltpu.VMEM((rows, columns), BF16),
            pltpu.VMEM((2, columns, rows), BF16),
            pltpu.VMEM((2, columns, rows), BF16),
            pltpu.VMEM(spread_dp.shape, F32),
            pltpu.SemaphoreType.DMA((heads // GROUP + 1, 4)),
        ],
    )(qn, g, qt, gt, kv, near, far_k, far_v, side, unit, inverse, terms, q_row)
    from_far = swap(to_far, 1)
    from_near = swap(to_near, 0)
    k_grad, v_grad, inverse_gain = call(
        finish_kernel,
        [far_away(flat), far_away(flat), like(1, width, dtype=F32)],
        rows * columns * 40,
        out_specs=[hbm, hbm, vmem],
        scratch=[
            pltpu.VMEM((rows, columns), BF16),
            pltpu.VMEM((rows, columns), BF16),
            pltpu.SemaphoreType.DMA((heads // STEP, 2)),
        ],
    )(kt, own, from_far, from_near, k_row)
    spread_seq = like(lax.axis_size("seq"), 1, width, dtype=F32)
    (spread,) = call(combine_kernel, [spread_seq], COMBINE)(exchange(spread, "dp"))
    parts = exchange(spread, "seq")
    gains = [like(1, width, dtype=F32)] * 2
    q_gain_grad, k_gain_grad = call(gain_kernel, gains, 0)(parts, q_row, inverse_gain)
    return (
        out[None],
        q_grad[None],
        k_grad[None],
        v_grad[None],
        q_gain_grad[0],
        k_gain_grad[0],
    )


def solution(mesh):
    tokens = P("dp", "seq", None)
    return jax.shard_map(
        shards,
        mesh=mesh,
        in_specs=(tokens, tokens, tokens, tokens, P(), P(), P(), P()),
        out_specs=(tokens, tokens, tokens, tokens, P(), P()),
        check_vma=False,
    )
```

```python
import math

import jax
import jax.numpy as jnp
from jax import lax
from jax.experimental import pallas as pl
from jax.experimental.pallas import tpu as pltpu
from jax.sharding import PartitionSpec as P

TILE = 64
REACH = 2
EPS = 1e-06
GROUP = 6
STEP = 6
IDLE = 5 * 10**9
COMBINE = 30 * 10**9
NT = (((1,), (1,)), ((), ()))
NN = (((1,), (0,)), ((), ()))
F32 = jnp.float32
BF16 = jnp.bfloat16


def dot(a, b, dims):
    return lax.dot_general(a, b, dims, preferred_element_type=F32)


def inverse_spread(rows, axis):
    return lax.rsqrt(jnp.mean(rows * rows, axis=axis, keepdims=True) + EPS)


def swap(block, parity):
    size = lax.axis_size("seq")
    route = [(i, i + 1 if i % 2 == parity else i - 1) for i in range(size)]
    return lax.ppermute(block, "seq", [(i, j) for i, j in route if 0 <= j < size])


def head_columns(ref, width):
    return [slice(h * width, (h + 1) * width) for h in range(ref.shape[-1] // width)]


def window_mask(offsets_t, counts_t, identity, position, t, rows):
    slots, heads = offsets_t.shape
    ntiles = counts_t.shape[1]
    tiles = rows // TILE
    lane = lax.broadcasted_iota(jnp.int32, (heads, 3 * rows), 1)
    side = 1 - 2 * lax.rem(position, 2)
    block = (lax.div(lane, rows) - 1) * side
    slot = block * tiles + lax.div(lax.rem(lane, rows), TILE) - t + REACH
    rank = jnp.zeros((heads, 3 * rows), F32)
    for s in range(slots):
        row = jnp.broadcast_to(offsets_t[s : s + 1, :], (heads, heads)).astype(F32)
        own = jnp.sum(row * identity, axis=1, keepdims=True)
        rank = rank + jnp.where(own == slot.astype(F32), float(s), 0.0)
    here = position * tiles + t
    tile = lax.broadcasted_iota(jnp.int32, (heads, ntiles), 1)
    used = jnp.sum(jnp.where(tile == here, counts_t.astype(F32), 0.0), axis=1, keepdims=True)
    key = here + slot - REACH
    inside = (slot >= 0) & (slot < slots) & (key >= 0) & (key < ntiles)
    return jnp.where(inside & ((slot == REACH) | (rank < used)), 1.0, 0.0)


def masked_terms(scores, scale, mask_ref, h, first):
    rows, wide = scores.shape
    mask = jnp.concatenate(
        [
            jnp.broadcast_to(mask_ref[t, h : h + 1, first : first + wide], (TILE, wide))
            for t in range(rows // TILE)
        ],
        axis=0,
    )
    return jnp.exp2(scores * (scale * math.log2(math.e))) * mask


def normal(raw, gain):
    rows = raw.astype(F32)
    return (rows * inverse_spread(rows, 1) * gain).astype(BF16)


def identity_kernel(identity_ref):
    size = identity_ref.shape[0]
    line = lax.broadcasted_iota(jnp.int32, (size, size), 0)
    identity_ref[...] = jnp.where(line == lax.broadcasted_iota(jnp.int32, (size, size), 1), 1.0, 0.0)


def prepare_kernel(
    q_ref, k_ref, v_ref, g_ref, offsets_ref, counts_ref, identity_ref, qgain_ref, kgain_ref,
    qn_ref, qt_ref, gt_ref, kv_ref, kt_ref, unit_ref, inverse_ref, own_ref, mask_ref,
):
    width = qgain_ref.shape[1]
    rows = q_ref.shape[0]
    scale = width ** (-0.5)
    q_gain = qgain_ref[...]
    k_gain = kgain_ref[...]
    position = lax.axis_index("seq")
    heads = offsets_ref.shape[1]
    identity = identity_ref[:heads, :heads]
    for t in range(rows // TILE):
        mask_ref[t] = window_mask(offsets_ref[...], counts_ref[...], identity, position, t, rows)
    for h, cols in enumerate(head_columns(q_ref, width)):
        q = q_ref[:, cols].astype(F32)
        inverse = inverse_spread(q, 1)
        unit = q * inverse
        unit_ref[:, cols] = unit
        inverse_ref[:, cols] = jnp.broadcast_to(inverse, (rows, width))
        qn = (unit * q_gain).astype(BF16)
        qn_ref[:, cols] = qn
        qt_ref[cols, :] = qn.T
        grads = g_ref[:, cols]
        gt_ref[cols, :] = grads.T
        raw = k_ref[:, cols]
        kt_ref[cols, :] = raw.T
        kn = normal(raw, k_gain)
        vals = v_ref[:, cols]
        kv_ref[0, :, cols] = kn
        kv_ref[1, :, cols] = vals
        own_ref[0, :, cols] = masked_terms(dot(qn, kn, NT), scale, mask_ref, h, rows)
        own_ref[1, :, cols] = dot(grads, vals, NT)


def far_kernel(k_ref, gain_ref, kn_ref):
    gain = gain_ref[...]
    for cols in head_columns(k_ref, gain_ref.shape[1]):
        kn_ref[:, cols] = normal(k_ref[:, cols], gain)


def side_kernel(
    qn_ref, g_ref, gt_ref, near_ref, fk_ref, mask_ref, own_ref, probs_ref, dprob_ref, far_v_ref, own_v_ref, near_v_ref
):
    rows = qn_ref.shape[0]
    width = gt_ref.shape[0] // mask_ref.shape[1]
    scale = width ** (-0.5)
    for h, cols in enumerate(head_columns(qn_ref, width)):
        scores = dot(qn_ref[:, cols], jnp.concatenate([fk_ref[:, cols], near_ref[0, :, cols]], axis=0), NT)
        dprob_ref[:, cols] = dot(g_ref[:, cols], near_ref[1, :, cols], NT)
        terms = [
            masked_terms(scores[:, :rows], scale, mask_ref, h, 0),
            own_ref[0, :, cols],
            masked_terms(scores[:, rows:], scale, mask_ref, h, 2 * rows),
        ]
        inverse = 1.0 / jnp.sum(terms[0] + terms[1] + terms[2], axis=1, keepdims=True)
        probs = [term * inverse for term in terms]
        for i, p in enumerate(probs):
            probs_ref[i, :, cols] = p
        weights = jnp.concatenate([p.astype(BF16) for p in probs], axis=1)
        val_t = dot(gt_ref[cols, :], weights, NN).astype(BF16)
        for i, ref in enumerate([far_v_ref, own_v_ref, near_v_ref]):
            ref[cols, :] = val_t[:, i * rows : (i + 1) * rows]


def attend_kernel(
    g_ref, qt_ref, kv_ref, near_ref, fk_ref, fv_ref, probs_ref, dprob_ref, far_v_ref, near_v_ref,
    unit_ref, inverse_ref, terms_ref, qgain_ref,
    out_hbm, qgrad_hbm, own_ref, far_hbm, near_hbm, spread_hbm,
    out_ref, qgrad_ref, to_far_ref, to_near_ref, spread_ref, sems,
):
    width = qgain_ref.shape[1]
    rows = g_ref.shape[0]
    scale = width ** (-0.5)
    q_gain = qgain_ref[...]
    heads = head_columns(g_ref, width)
    count = len(heads)
    copies = [
        pltpu.make_async_copy(far_v_ref, far_hbm.at[1], sems.at[count // GROUP, 1]),
        pltpu.make_async_copy(near_v_ref, near_hbm.at[1], sems.at[count // GROUP, 2]),
    ]
    for copy in copies:
        copy.start()

    def first_stage(h):
        return (dot(g_ref[:, heads[h]], fv_ref[:, heads[h]], NT),)

    def middle_stage(h, dprob):
        cols = heads[h]
        probs = [probs_ref[i, :, cols] for i in range(3)]
        dprobs = [dprob, terms_ref[1, :, cols], dprob_ref[:, cols]]
        delta = jnp.sum(
            probs[0] * dprobs[0] + probs[1] * dprobs[1] + probs[2] * dprobs[2], axis=1, keepdims=True
        )
        dscore = [(p * (d - delta)).astype(BF16) for p, d in zip(probs, dprobs)]
        weights = [p.astype(BF16) for p in probs]
        return jnp.concatenate(dscore, axis=1), jnp.concatenate(weights, axis=1)

    def last_stage(h, dscore, weights, total_gain):
        cols = heads[h]
        keys = jnp.concatenate([fk_ref[:, cols], kv_ref[0, :, cols], near_ref[0, :, cols]], axis=0)
        vals = jnp.concatenate([fv_ref[:, cols], kv_ref[1, :, cols], near_ref[1, :, cols]], axis=0)
        grad_qn = dot(dscore, keys, NN) * scale
        out_ref[:, cols] = dot(weights, vals, NN).astype(BF16)
        key_t = dot(qt_ref[cols, :], dscore, NN) * scale
        own_ref[cols, :] = key_t[:, rows : 2 * rows].astype(BF16)
        to_far_ref[cols, :] = key_t[:, :rows].astype(BF16)
        to_near_ref[cols, :] = key_t[:, 2 * rows :].astype(BF16)
        unit = unit_ref[:, cols]
        product = grad_qn * unit
        mean = jnp.mean(product * q_gain, axis=1, keepdims=True)
        qgrad_ref[:, cols] = ((grad_qn * q_gain - unit * mean) * inverse_ref[:, cols]).astype(BF16)
        if h % GROUP == GROUP - 1:
            i = h // GROUP
            span = slice(heads[h - GROUP + 1].start, cols.stop)
            pairs = [
                (to_far_ref.at[span, :], far_hbm.at[0, span, :]),
                (to_near_ref.at[span, :], near_hbm.at[0, span, :]),
                (out_ref.at[:, span], out_hbm.at[:, span]),
                (qgrad_ref.at[:, span], qgrad_hbm.at[:, span]),
            ]
            for j, (here, there) in enumerate(pairs):
                copy = pltpu.make_async_copy(here, there, sems.at[i, j])
                copy.start()
                copies.append(copy)
        return total_gain + product

    total_gain = jnp.zeros((rows, width), F32)
    ahead = first_stage(0)
    behind = None
    for h in range(count):
        now = ahead
        if h + 1 < count:
            ahead = first_stage(h + 1)
        now = middle_stage(h, *now)
        if behind is not None:
            total_gain = last_stage(h - 1, *behind, total_gain)
        behind = now
    total_gain = last_stage(count - 1, *behind, total_gain)
    sums = jnp.sum(total_gain, axis=0, keepdims=True)
    spread_ref[...] = jnp.broadcast_to(sums[None], spread_ref.shape)
    copies.append(pltpu.make_async_copy(spread_ref, spread_hbm, sems.at[count // GROUP, 0]))
    copies[-1].start()
    for copy in copies:
        copy.wait()


def finish_kernel(
    kt_ref, own_k_ref, own_v_ref, far_ref, near_ref, gain_ref, kgrad_hbm, vgrad_hbm, inverse_ref, kgrad_ref, vgrad_ref, sems
):
    width = gain_ref.shape[1]
    row = gain_ref[...]
    inverse_ref[...] = 1.0 / row
    line = lax.broadcasted_iota(jnp.int32, (width, width), 0)
    diagonal = line == lax.broadcasted_iota(jnp.int32, (width, width), 1)
    gain = jnp.sum(jnp.where(diagonal, jnp.broadcast_to(row, (width, width)), 0.0), axis=1, keepdims=True)
    heads = head_columns(kgrad_ref, width)
    copies = []
    for h, cols in enumerate(heads):

        def total(i):
            own = (own_k_ref, own_v_ref)[i][cols, :].astype(F32)
            return own + far_ref[i, cols, :].astype(F32) + near_ref[i, cols, :].astype(F32)

        k = kt_ref[cols, :].astype(F32)
        inverse = inverse_spread(k, 0)
        unit = k * inverse
        scaled = total(0) * gain
        mean = jnp.mean(scaled * unit, axis=0, keepdims=True)
        kgrad_ref[:, cols] = ((scaled - unit * mean) * inverse).astype(BF16).T
        vgrad_ref[:, cols] = total(1).astype(BF16).T
        if h % STEP == STEP - 1:
            i = h // STEP
            span = slice(heads[h - STEP + 1].start, cols.stop)
            for j, (here, there) in enumerate([(kgrad_ref, kgrad_hbm), (vgrad_ref, vgrad_hbm)]):
                copies.append(pltpu.make_async_copy(here.at[:, span], there.at[:, span], sems.at[i, j]))
                copies[-1].start()
    for copy in copies:
        copy.wait()


def combine_kernel(parts_ref, spread_ref):
    spread_ref[...] = jnp.broadcast_to(jnp.sum(parts_ref[...], axis=0, keepdims=True), spread_ref.shape)


def gain_kernel(parts_ref, q_ref, inverse_ref, qgain_ref, kgain_ref):
    total = jnp.sum(parts_ref[...], axis=0)
    qgain_ref[...] = total
    kgain_ref[...] = total * q_ref[...] * inverse_ref[...]


def call(body, out_shape, flops, in_specs=None, out_specs=None, scratch=(), vmem=24):
    whole = pl.BlockSpec(memory_space=pltpu.VMEM)

    def run(*args):
        return pl.pallas_call(
            body,
            in_specs=in_specs or [whole] * len(args),
            out_specs=out_specs or [whole] * len(out_shape),
            out_shape=out_shape,
            scratch_shapes=scratch,
            compiler_params=pltpu.CompilerParams(vmem_limit_bytes=vmem * 1024 * 1024),
            cost_estimate=pl.CostEstimate(flops=flops, bytes_accessed=4 << 20, transcendentals=0),
        )(*args)

    return run


def exchange(parts, axis):
    return lax.all_to_all(parts, axis, 0, 0)


def shards(q_raw, k_raw, values, d_out, q_gain, k_gain, offsets, counts):
    rows, columns = q_raw.shape[1:]
    width = q_gain.shape[0]
    heads = offsets.shape[0]
    q, k, v, g = q_raw[0], k_raw[0], values[0], d_out[0]
    q_row, k_row = q_gain[None], k_gain[None]

    def like(*shape, dtype=BF16):
        return jax.ShapeDtypeStruct(shape, dtype)

    def far_away(shape):
        return pltpu.HBM(shape.shape, shape.dtype)

    hbm = pl.BlockSpec(memory_space=pltpu.HBM)
    vmem = pl.BlockSpec(memory_space=pltpu.VMEM)
    products = 2 * rows * rows * columns
    flat = like(rows, columns)
    turned = like(columns, rows)
    part = like(2, columns, rows)

    far_k, far_v = swap(k, 1), swap(v, 1)
    (identity,) = call(identity_kernel, [like(width, width, dtype=F32)], IDLE)()
    wide = like(rows, columns, dtype=F32)
    qn, qt, gt, kv, kt, unit, inverse, terms, mask = call(
        prepare_kernel,
        [flat, turned, turned, like(2, rows, columns), turned, wide, wide]
        + [like(2, rows, columns, dtype=F32), like(rows // TILE, heads, 3 * rows, dtype=F32)],
        2 * products,
    )(q, k, v, g, offsets.T, counts.T, identity, q_row, k_row)
    near = swap(kv, 0)
    (far_k,) = call(far_kernel, [flat], 2 * IDLE)(far_k, k_row)
    probs, dprob, far_v_part, own_v_part, near_v_part = call(
        side_kernel,
        [like(3, rows, columns, dtype=F32), wide, turned, turned, turned],
        6 * products,
    )(qn, g, gt, near, far_k, mask, terms)
    spread_dp = like(lax.axis_size("dp"), 1, width, dtype=F32)
    out, q_grad, own_k_part, to_far, to_near, spread = call(
        attend_kernel,
        [far_away(flat), far_away(flat), turned, far_away(part), far_away(part), far_away(spread_dp)],
        11 * products,
        out_specs=[hbm, hbm, vmem, hbm, hbm, hbm],
        scratch=[
            pltpu.VMEM((rows, columns), BF16),
            pltpu.VMEM((rows, columns), BF16),
            pltpu.VMEM((columns, rows), BF16),
            pltpu.VMEM((columns, rows), BF16),
            pltpu.VMEM(spread_dp.shape, F32),
            pltpu.SemaphoreType.DMA((heads // GROUP + 1, 4)),
        ],
    )(g, qt, kv, near, far_k, far_v, probs, dprob, far_v_part, near_v_part, unit, inverse, terms, q_row)
    from_far = swap(to_far, 1)
    from_near = swap(to_near, 0)
    k_grad, v_grad, inverse_gain = call(
        finish_kernel,
        [far_away(flat), far_away(flat), like(1, width, dtype=F32)],
        rows * columns * 40,
        out_specs=[hbm, hbm, vmem],
        scratch=[
            pltpu.VMEM((rows, columns), BF16),
            pltpu.VMEM((rows, columns), BF16),
            pltpu.SemaphoreType.DMA((heads // STEP, 2)),
        ],
    )(kt, own_k_part, own_v_part, from_far, from_near, k_row)
    spread_seq = like(lax.axis_size("seq"), 1, width, dtype=F32)
    (spread,) = call(combine_kernel, [spread_seq], COMBINE)(exchange(spread, "dp"))
    parts = exchange(spread, "seq")
    gains = [like(1, width, dtype=F32)] * 2
    q_gain_grad, k_gain_grad = call(gain_kernel, gains, 0)(parts, q_row, inverse_gain)
    return (
        out[None],
        q_grad[None],
        k_grad[None],
        v_grad[None],
        q_gain_grad[0],
        k_gain_grad[0],
    )


def solution(mesh):
    tokens = P("dp", "seq", None)
    return jax.shard_map(
        shards,
        mesh=mesh,
        in_specs=(tokens, tokens, tokens, tokens, P(), P(), P(), P()),
        out_specs=(tokens, tokens, tokens, tokens, P(), P()),
        check_vma=False,
    )
```

```python
import math

import jax
import jax.numpy as jnp
from jax import lax
from jax.experimental import pallas as pl
from jax.experimental.pallas import tpu as pltpu
from jax.sharding import PartitionSpec as P

TILE = 64
REACH = 2
EPS = 1e-06
GROUP = 6
STEP = 6
IDLE = 5 * 10**9
COMBINE = 30 * 10**9
NT = (((1,), (1,)), ((), ()))
NN = (((1,), (0,)), ((), ()))
F32 = jnp.float32
BF16 = jnp.bfloat16


def dot(a, b, dims):
    return lax.dot_general(a, b, dims, preferred_element_type=F32)


def inverse_spread(rows, axis):
    return lax.rsqrt(jnp.mean(rows * rows, axis=axis, keepdims=True) + EPS)


def swap(block, parity):
    size = lax.axis_size("seq")
    route = [(i, i + 1 if i % 2 == parity else i - 1) for i in range(size)]
    return lax.ppermute(block, "seq", [(i, j) for i, j in route if 0 <= j < size])


def head_columns(ref, width):
    return [slice(h * width, (h + 1) * width) for h in range(ref.shape[-1] // width)]


def window_mask(offsets_t, counts_t, identity, position, t, rows):
    slots, heads = offsets_t.shape
    ntiles = counts_t.shape[1]
    tiles = rows // TILE
    lane = lax.broadcasted_iota(jnp.int32, (heads, 3 * rows), 1)
    side = 1 - 2 * lax.rem(position, 2)
    block = (lax.div(lane, rows) - 1) * side
    slot = block * tiles + lax.div(lax.rem(lane, rows), TILE) - t + REACH
    rank = jnp.zeros((heads, 3 * rows), F32)
    for s in range(slots):
        row = jnp.broadcast_to(offsets_t[s : s + 1, :], (heads, heads)).astype(F32)
        own = jnp.sum(row * identity, axis=1, keepdims=True)
        rank = rank + jnp.where(own == slot.astype(F32), float(s), 0.0)
    here = position * tiles + t
    tile = lax.broadcasted_iota(jnp.int32, (heads, ntiles), 1)
    used = jnp.sum(jnp.where(tile == here, counts_t.astype(F32), 0.0), axis=1, keepdims=True)
    key = here + slot - REACH
    inside = (slot >= 0) & (slot < slots) & (key >= 0) & (key < ntiles)
    return jnp.where(inside & ((slot == REACH) | (rank < used)), 1.0, 0.0)


def masked_terms(scores, scale, mask_ref, h, first):
    rows, wide = scores.shape
    mask = jnp.concatenate(
        [
            jnp.broadcast_to(mask_ref[t, h : h + 1, first : first + wide], (TILE, wide))
            for t in range(rows // TILE)
        ],
        axis=0,
    )
    return jnp.exp2(scores * (scale * math.log2(math.e))) * mask


def normal(raw, gain):
    rows = raw.astype(F32)
    return (rows * inverse_spread(rows, 1) * gain).astype(BF16)


def identity_kernel(identity_ref):
    size = identity_ref.shape[0]
    line = lax.broadcasted_iota(jnp.int32, (size, size), 0)
    identity_ref[...] = jnp.where(line == lax.broadcasted_iota(jnp.int32, (size, size), 1), 1.0, 0.0)


def prepare_kernel(
    q_ref, k_ref, v_ref, g_ref, offsets_ref, counts_ref, identity_ref, qgain_ref, kgain_ref,
    qn_ref, qt_ref, gt_ref, kv_ref, kt_ref, unit_ref, inverse_ref, own_ref, mask_ref,
):
    width = qgain_ref.shape[1]
    rows = q_ref.shape[0]
    scale = width ** (-0.5)
    q_gain = qgain_ref[...]
    k_gain = kgain_ref[...]
    position = lax.axis_index("seq")
    heads = offsets_ref.shape[1]
    identity = identity_ref[:heads, :heads]
    for t in range(rows // TILE):
        mask_ref[t] = window_mask(offsets_ref[...], counts_ref[...], identity, position, t, rows)
    for h, cols in enumerate(head_columns(q_ref, width)):
        q = q_ref[:, cols].astype(F32)
        inverse = inverse_spread(q, 1)
        unit = q * inverse
        unit_ref[:, cols] = unit
        inverse_ref[:, cols] = jnp.broadcast_to(inverse, (rows, width))
        qn = (unit * q_gain).astype(BF16)
        qn_ref[:, cols] = qn
        qt_ref[cols, :] = qn.T
        grads = g_ref[:, cols]
        gt_ref[cols, :] = grads.T
        raw = k_ref[:, cols]
        kt_ref[cols, :] = raw.T
        kn = normal(raw, k_gain)
        vals = v_ref[:, cols]
        kv_ref[0, :, cols] = kn
        kv_ref[1, :, cols] = vals
        own_ref[0, :, cols] = masked_terms(dot(qn, kn, NT), scale, mask_ref, h, rows)
        own_ref[1, :, cols] = dot(grads, vals, NT)


def far_kernel(k_ref, gain_ref, kn_ref):
    gain = gain_ref[...]
    for cols in head_columns(k_ref, gain_ref.shape[1]):
        kn_ref[:, cols] = normal(k_ref[:, cols], gain)


def side_kernel(
    qn_ref, g_ref, gt_ref, near_ref, fk_ref, mask_ref, own_ref, probs_ref, dprob_ref, far_v_ref, own_v_ref, near_v_ref
):
    rows = qn_ref.shape[0]
    width = gt_ref.shape[0] // mask_ref.shape[1]
    scale = width ** (-0.5)
    heads = head_columns(qn_ref, width)
    count = len(heads)

    def first_stage(h):
        cols = heads[h]
        return dot(qn_ref[:, cols], jnp.concatenate([fk_ref[:, cols], near_ref[0, :, cols]], axis=0), NT)

    def middle_stage(h, scores):
        cols = heads[h]
        terms = [
            masked_terms(scores[:, :rows], scale, mask_ref, h, 0),
            own_ref[0, :, cols],
            masked_terms(scores[:, rows:], scale, mask_ref, h, 2 * rows),
        ]
        inverse = 1.0 / jnp.sum(terms[0] + terms[1] + terms[2], axis=1, keepdims=True)
        probs = [term * inverse for term in terms]
        for i, p in enumerate(probs):
            probs_ref[i, :, cols] = p
        return jnp.concatenate([p.astype(BF16) for p in probs], axis=1)

    def last_stage(h, weights):
        cols = heads[h]
        dprob_ref[:, cols] = dot(g_ref[:, cols], near_ref[1, :, cols], NT)
        val_t = dot(gt_ref[cols, :], weights, NN).astype(BF16)
        for i, ref in enumerate([far_v_ref, own_v_ref, near_v_ref]):
            ref[cols, :] = val_t[:, i * rows : (i + 1) * rows]

    ahead = first_stage(0)
    behind = None
    for h in range(count):
        now = ahead
        if h + 1 < count:
            ahead = first_stage(h + 1)
        now = middle_stage(h, now)
        if behind is not None:
            last_stage(h - 1, behind)
        behind = now
    last_stage(count - 1, behind)


def attend_kernel(
    g_ref, qt_ref, kv_ref, near_ref, fk_ref, fv_ref, probs_ref, dprob_ref, far_v_ref, near_v_ref,
    unit_ref, inverse_ref, terms_ref, qgain_ref,
    out_hbm, qgrad_hbm, own_ref, far_hbm, near_hbm, spread_hbm,
    out_ref, qgrad_ref, to_far_ref, to_near_ref, spread_ref, sems,
):
    width = qgain_ref.shape[1]
    rows = g_ref.shape[0]
    scale = width ** (-0.5)
    q_gain = qgain_ref[...]
    heads = head_columns(g_ref, width)
    count = len(heads)
    copies = [
        pltpu.make_async_copy(far_v_ref, far_hbm.at[1], sems.at[count // GROUP, 1]),
        pltpu.make_async_copy(near_v_ref, near_hbm.at[1], sems.at[count // GROUP, 2]),
    ]
    for copy in copies:
        copy.start()

    def first_stage(h):
        return (dot(g_ref[:, heads[h]], fv_ref[:, heads[h]], NT),)

    def middle_stage(h, dprob):
        cols = heads[h]
        probs = [probs_ref[i, :, cols] for i in range(3)]
        dprobs = [dprob, terms_ref[1, :, cols], dprob_ref[:, cols]]
        delta = jnp.sum(
            probs[0] * dprobs[0] + probs[1] * dprobs[1] + probs[2] * dprobs[2], axis=1, keepdims=True
        )
        dscore = [(p * (d - delta)).astype(BF16) for p, d in zip(probs, dprobs)]
        weights = [p.astype(BF16) for p in probs]
        return jnp.concatenate(dscore, axis=1), jnp.concatenate(weights, axis=1)

    def last_stage(h, dscore, weights, total_gain):
        cols = heads[h]
        keys = jnp.concatenate([fk_ref[:, cols], kv_ref[0, :, cols], near_ref[0, :, cols]], axis=0)
        vals = jnp.concatenate([fv_ref[:, cols], kv_ref[1, :, cols], near_ref[1, :, cols]], axis=0)
        grad_qn = dot(dscore, keys, NN) * scale
        out_ref[:, cols] = dot(weights, vals, NN).astype(BF16)
        key_t = dot(qt_ref[cols, :], dscore, NN) * scale
        own_ref[cols, :] = key_t[:, rows : 2 * rows].astype(BF16)
        to_far_ref[cols, :] = key_t[:, :rows].astype(BF16)
        to_near_ref[cols, :] = key_t[:, 2 * rows :].astype(BF16)
        unit = unit_ref[:, cols]
        product = grad_qn * unit
        mean = jnp.mean(product * q_gain, axis=1, keepdims=True)
        qgrad_ref[:, cols] = ((grad_qn * q_gain - unit * mean) * inverse_ref[:, cols]).astype(BF16)
        if h % GROUP == GROUP - 1:
            i = h // GROUP
            span = slice(heads[h - GROUP + 1].start, cols.stop)
            pairs = [
                (to_far_ref.at[span, :], far_hbm.at[0, span, :]),
                (to_near_ref.at[span, :], near_hbm.at[0, span, :]),
                (out_ref.at[:, span], out_hbm.at[:, span]),
                (qgrad_ref.at[:, span], qgrad_hbm.at[:, span]),
            ]
            for j, (here, there) in enumerate(pairs):
                copy = pltpu.make_async_copy(here, there, sems.at[i, j])
                copy.start()
                copies.append(copy)
        return total_gain + product

    total_gain = jnp.zeros((rows, width), F32)
    ahead = first_stage(0)
    behind = None
    for h in range(count):
        now = ahead
        if h + 1 < count:
            ahead = first_stage(h + 1)
        now = middle_stage(h, *now)
        if behind is not None:
            total_gain = last_stage(h - 1, *behind, total_gain)
        behind = now
    total_gain = last_stage(count - 1, *behind, total_gain)
    sums = jnp.sum(total_gain, axis=0, keepdims=True)
    spread_ref[...] = jnp.broadcast_to(sums[None], spread_ref.shape)
    copies.append(pltpu.make_async_copy(spread_ref, spread_hbm, sems.at[count // GROUP, 0]))
    copies[-1].start()
    for copy in copies:
        copy.wait()


def finish_kernel(
    kt_ref, own_k_ref, own_v_ref, far_ref, near_ref, gain_ref, kgrad_hbm, vgrad_hbm, inverse_ref, kgrad_ref, vgrad_ref, sems
):
    width = gain_ref.shape[1]
    row = gain_ref[...]
    inverse_ref[...] = 1.0 / row
    line = lax.broadcasted_iota(jnp.int32, (width, width), 0)
    diagonal = line == lax.broadcasted_iota(jnp.int32, (width, width), 1)
    gain = jnp.sum(jnp.where(diagonal, jnp.broadcast_to(row, (width, width)), 0.0), axis=1, keepdims=True)
    heads = head_columns(kgrad_ref, width)
    copies = []
    for h, cols in enumerate(heads):

        def total(i):
            own = (own_k_ref, own_v_ref)[i][cols, :].astype(F32)
            return own + far_ref[i, cols, :].astype(F32) + near_ref[i, cols, :].astype(F32)

        k = kt_ref[cols, :].astype(F32)
        inverse = inverse_spread(k, 0)
        unit = k * inverse
        scaled = total(0) * gain
        mean = jnp.mean(scaled * unit, axis=0, keepdims=True)
        kgrad_ref[:, cols] = ((scaled - unit * mean) * inverse).astype(BF16).T
        vgrad_ref[:, cols] = total(1).astype(BF16).T
        if h % STEP == STEP - 1:
            i = h // STEP
            span = slice(heads[h - STEP + 1].start, cols.stop)
            for j, (here, there) in enumerate([(kgrad_ref, kgrad_hbm), (vgrad_ref, vgrad_hbm)]):
                copies.append(pltpu.make_async_copy(here.at[:, span], there.at[:, span], sems.at[i, j]))
                copies[-1].start()
    for copy in copies:
        copy.wait()


def combine_kernel(parts_ref, spread_ref):
    spread_ref[...] = jnp.broadcast_to(jnp.sum(parts_ref[...], axis=0, keepdims=True), spread_ref.shape)


def gain_kernel(parts_ref, q_ref, inverse_ref, qgain_ref, kgain_ref):
    total = jnp.sum(parts_ref[...], axis=0)
    qgain_ref[...] = total
    kgain_ref[...] = total * q_ref[...] * inverse_ref[...]


def call(body, out_shape, flops, in_specs=None, out_specs=None, scratch=(), vmem=24):
    whole = pl.BlockSpec(memory_space=pltpu.VMEM)

    def run(*args):
        return pl.pallas_call(
            body,
            in_specs=in_specs or [whole] * len(args),
            out_specs=out_specs or [whole] * len(out_shape),
            out_shape=out_shape,
            scratch_shapes=scratch,
            compiler_params=pltpu.CompilerParams(vmem_limit_bytes=vmem * 1024 * 1024),
            cost_estimate=pl.CostEstimate(flops=flops, bytes_accessed=4 << 20, transcendentals=0),
        )(*args)

    return run


def exchange(parts, axis):
    return lax.all_to_all(parts, axis, 0, 0)


def shards(q_raw, k_raw, values, d_out, q_gain, k_gain, offsets, counts):
    rows, columns = q_raw.shape[1:]
    width = q_gain.shape[0]
    heads = offsets.shape[0]
    q, k, v, g = q_raw[0], k_raw[0], values[0], d_out[0]
    q_row, k_row = q_gain[None], k_gain[None]

    def like(*shape, dtype=BF16):
        return jax.ShapeDtypeStruct(shape, dtype)

    def far_away(shape):
        return pltpu.HBM(shape.shape, shape.dtype)

    hbm = pl.BlockSpec(memory_space=pltpu.HBM)
    vmem = pl.BlockSpec(memory_space=pltpu.VMEM)
    products = 2 * rows * rows * columns
    flat = like(rows, columns)
    turned = like(columns, rows)
    part = like(2, columns, rows)

    far_k, far_v = swap(k, 1), swap(v, 1)
    (identity,) = call(identity_kernel, [like(width, width, dtype=F32)], IDLE)()
    wide = like(rows, columns, dtype=F32)
    qn, qt, gt, kv, kt, unit, inverse, terms, mask = call(
        prepare_kernel,
        [flat, turned, turned, like(2, rows, columns), turned, wide, wide]
        + [like(2, rows, columns, dtype=F32), like(rows // TILE, heads, 3 * rows, dtype=F32)],
        2 * products,
    )(q, k, v, g, offsets.T, counts.T, identity, q_row, k_row)
    near = swap(kv, 0)
    (far_k,) = call(far_kernel, [flat], 2 * IDLE)(far_k, k_row)
    probs, dprob, far_v_part, own_v_part, near_v_part = call(
        side_kernel,
        [like(3, rows, columns, dtype=F32), wide, turned, turned, turned],
        6 * products,
    )(qn, g, gt, near, far_k, mask, terms)
    spread_dp = like(lax.axis_size("dp"), 1, width, dtype=F32)
    out, q_grad, own_k_part, to_far, to_near, spread = call(
        attend_kernel,
        [far_away(flat), far_away(flat), turned, far_away(part), far_away(part), far_away(spread_dp)],
        11 * products,
        out_specs=[hbm, hbm, vmem, hbm, hbm, hbm],
        scratch=[
            pltpu.VMEM((rows, columns), BF16),
            pltpu.VMEM((rows, columns), BF16),
            pltpu.VMEM((columns, rows), BF16),
            pltpu.VMEM((columns, rows), BF16),
            pltpu.VMEM(spread_dp.shape, F32),
            pltpu.SemaphoreType.DMA((heads // GROUP + 1, 4)),
        ],
    )(g, qt, kv, near, far_k, far_v, probs, dprob, far_v_part, near_v_part, unit, inverse, terms, q_row)
    from_far = swap(to_far, 1)
    from_near = swap(to_near, 0)
    k_grad, v_grad, inverse_gain = call(
        finish_kernel,
        [far_away(flat), far_away(flat), like(1, width, dtype=F32)],
        rows * columns * 40,
        out_specs=[hbm, hbm, vmem],
        scratch=[
            pltpu.VMEM((rows, columns), BF16),
            pltpu.VMEM((rows, columns), BF16),
            pltpu.SemaphoreType.DMA((heads // STEP, 2)),
        ],
    )(kt, own_k_part, own_v_part, from_far, from_near, k_row)
    spread_seq = like(lax.axis_size("seq"), 1, width, dtype=F32)
    (spread,) = call(combine_kernel, [spread_seq], COMBINE)(exchange(spread, "dp"))
    parts = exchange(spread, "seq")
    gains = [like(1, width, dtype=F32)] * 2
    q_gain_grad, k_gain_grad = call(gain_kernel, gains, 0)(parts, q_row, inverse_gain)
    return (
        out[None],
        q_grad[None],
        k_grad[None],
        v_grad[None],
        q_gain_grad[0],
        k_gain_grad[0],
    )


def solution(mesh):
    tokens = P("dp", "seq", None)
    return jax.shard_map(
        shards,
        mesh=mesh,
        in_specs=(tokens, tokens, tokens, tokens, P(), P(), P(), P()),
        out_specs=(tokens, tokens, tokens, tokens, P(), P()),
        check_vma=False,
    )
```

```python
import math

import jax
import jax.numpy as jnp
from jax import lax
from jax.experimental import pallas as pl
from jax.experimental.pallas import tpu as pltpu
from jax.sharding import PartitionSpec as P

TILE = 64
REACH = 2
EPS = 1e-06
GROUP = 6
STEP = 6
IDLE = 5 * 10**9
COMBINE = 30 * 10**9
NT = (((1,), (1,)), ((), ()))
NN = (((1,), (0,)), ((), ()))
F32 = jnp.float32
BF16 = jnp.bfloat16


def dot(a, b, dims):
    return lax.dot_general(a, b, dims, preferred_element_type=F32)


def inverse_spread(rows, axis):
    return lax.rsqrt(jnp.mean(rows * rows, axis=axis, keepdims=True) + EPS)


def swap(block, parity):
    size = lax.axis_size("seq")
    route = [(i, i + 1 if i % 2 == parity else i - 1) for i in range(size)]
    return lax.ppermute(block, "seq", [(i, j) for i, j in route if 0 <= j < size])


def head_columns(ref, width):
    return [slice(h * width, (h + 1) * width) for h in range(ref.shape[-1] // width)]


def window_mask(offsets_t, counts_t, identity, position, t, rows):
    slots, heads = offsets_t.shape
    ntiles = counts_t.shape[1]
    tiles = rows // TILE
    lane = lax.broadcasted_iota(jnp.int32, (heads, 3 * rows), 1)
    side = 1 - 2 * lax.rem(position, 2)
    block = (lax.div(lane, rows) - 1) * side
    slot = block * tiles + lax.div(lax.rem(lane, rows), TILE) - t + REACH
    rank = jnp.zeros((heads, 3 * rows), F32)
    for s in range(slots):
        row = jnp.broadcast_to(offsets_t[s : s + 1, :], (heads, heads)).astype(F32)
        own = jnp.sum(row * identity, axis=1, keepdims=True)
        rank = rank + jnp.where(own == slot.astype(F32), float(s), 0.0)
    here = position * tiles + t
    tile = lax.broadcasted_iota(jnp.int32, (heads, ntiles), 1)
    used = jnp.sum(jnp.where(tile == here, counts_t.astype(F32), 0.0), axis=1, keepdims=True)
    key = here + slot - REACH
    inside = (slot >= 0) & (slot < slots) & (key >= 0) & (key < ntiles)
    return jnp.where(inside & ((slot == REACH) | (rank < used)), 1.0, 0.0)


def masked_terms(scores, scale, mask_ref, h, first):
    rows, wide = scores.shape
    mask = jnp.concatenate(
        [
            jnp.broadcast_to(mask_ref[t, h : h + 1, first : first + wide], (TILE, wide))
            for t in range(rows // TILE)
        ],
        axis=0,
    )
    return jnp.exp2(scores * (scale * math.log2(math.e))) * mask


def normal(raw, gain):
    rows = raw.astype(F32)
    return (rows * inverse_spread(rows, 1) * gain).astype(BF16)


def identity_kernel(identity_ref):
    size = identity_ref.shape[0]
    line = lax.broadcasted_iota(jnp.int32, (size, size), 0)
    identity_ref[...] = jnp.where(line == lax.broadcasted_iota(jnp.int32, (size, size), 1), 1.0, 0.0)


def prepare_kernel(
    q_ref, k_ref, v_ref, g_ref, offsets_ref, counts_ref, identity_ref, qgain_ref, kgain_ref,
    qn_ref, qt_ref, gt_ref, kv_ref, kt_ref, unit_ref, inverse_ref, own_ref, mask_ref,
):
    width = qgain_ref.shape[1]
    rows = q_ref.shape[0]
    scale = width ** (-0.5)
    q_gain = qgain_ref[...]
    k_gain = kgain_ref[...]
    position = lax.axis_index("seq")
    heads = offsets_ref.shape[1]
    identity = identity_ref[:heads, :heads]
    for t in range(rows // TILE):
        mask_ref[t] = window_mask(offsets_ref[...], counts_ref[...], identity, position, t, rows)
    for h, cols in enumerate(head_columns(q_ref, width)):
        q = q_ref[:, cols].astype(F32)
        inverse = inverse_spread(q, 1)
        unit = q * inverse
        unit_ref[:, cols] = unit
        inverse_ref[:, cols] = jnp.broadcast_to(inverse, (rows, width))
        qn = (unit * q_gain).astype(BF16)
        qn_ref[:, cols] = qn
        qt_ref[cols, :] = qn.T
        grads = g_ref[:, cols]
        gt_ref[cols, :] = grads.T
        raw = k_ref[:, cols]
        kt_ref[cols, :] = raw.T
        kn = normal(raw, k_gain)
        vals = v_ref[:, cols]
        kv_ref[0, :, cols] = kn
        kv_ref[1, :, cols] = vals
        own_ref[0, :, cols] = masked_terms(dot(qn, kn, NT), scale, mask_ref, h, rows)
        own_ref[1, :, cols] = dot(grads, vals, NT)


def far_kernel(k_ref, gain_ref, kn_ref):
    gain = gain_ref[...]
    for cols in head_columns(k_ref, gain_ref.shape[1]):
        kn_ref[:, cols] = normal(k_ref[:, cols], gain)


def side_kernel(
    qn_ref, g_ref, gt_ref, near_ref, fk_ref, mask_ref, own_ref, probs_ref, dprob_ref, far_v_ref, own_v_ref, near_v_ref
):
    rows = qn_ref.shape[0]
    width = gt_ref.shape[0] // mask_ref.shape[1]
    scale = width ** (-0.5)
    heads = head_columns(qn_ref, width)
    count = len(heads)

    def first_stage(h):
        cols = heads[h]
        return dot(qn_ref[:, cols], jnp.concatenate([fk_ref[:, cols], near_ref[0, :, cols]], axis=0), NT)

    def middle_stage(h, scores):
        cols = heads[h]
        terms = [
            masked_terms(scores[:, :rows], scale, mask_ref, h, 0),
            own_ref[0, :, cols],
            masked_terms(scores[:, rows:], scale, mask_ref, h, 2 * rows),
        ]
        inverse = 1.0 / jnp.sum(terms[0] + terms[1] + terms[2], axis=1, keepdims=True)
        probs = [term * inverse for term in terms]
        for i, p in enumerate(probs):
            probs_ref[i, :, cols] = p
        return jnp.concatenate([p.astype(BF16) for p in probs], axis=1)

    def last_stage(h, weights):
        cols = heads[h]
        dprob_ref[:, cols] = dot(g_ref[:, cols], near_ref[1, :, cols], NT)
        val_t = dot(gt_ref[cols, :], weights, NN).astype(BF16)
        for i, ref in enumerate([far_v_ref, own_v_ref, near_v_ref]):
            ref[cols, :] = val_t[:, i * rows : (i + 1) * rows]

    ahead = first_stage(0)
    behind = None
    for h in range(count):
        now = ahead
        if h + 1 < count:
            ahead = first_stage(h + 1)
        now = middle_stage(h, now)
        if behind is not None:
            last_stage(h - 1, behind)
        behind = now
    last_stage(count - 1, behind)


def attend_kernel(
    g_ref, qt_ref, kv_ref, near_ref, fk_ref, fv_ref, probs_ref, dprob_ref, far_v_ref, near_v_ref,
    unit_ref, inverse_ref, terms_ref, qgain_ref,
    out_hbm, qgrad_hbm, own_ref, far_hbm, near_hbm, spread_hbm,
    out_ref, qgrad_ref, to_far_ref, to_near_ref, spread_ref, sems,
):
    width = qgain_ref.shape[1]
    rows = g_ref.shape[0]
    scale = width ** (-0.5)
    q_gain = qgain_ref[...]
    heads = head_columns(g_ref, width)
    count = len(heads)
    copies = [
        pltpu.make_async_copy(far_v_ref, far_hbm.at[1], sems.at[count // GROUP, 1]),
        pltpu.make_async_copy(near_v_ref, near_hbm.at[1], sems.at[count // GROUP, 2]),
    ]
    for copy in copies:
        copy.start()

    def first_stage(h):
        return (dot(g_ref[:, heads[h]], fv_ref[:, heads[h]], NT),)

    def middle_stage(h, dprob):
        cols = heads[h]
        probs = [probs_ref[i, :, cols] for i in range(3)]
        dprobs = [dprob, terms_ref[1, :, cols], dprob_ref[:, cols]]
        delta = jnp.sum(
            probs[0] * dprobs[0] + probs[1] * dprobs[1] + probs[2] * dprobs[2], axis=1, keepdims=True
        )
        dscore = [(p * (d - delta)).astype(BF16) for p, d in zip(probs, dprobs)]
        weights = [p.astype(BF16) for p in probs]
        return jnp.concatenate(dscore, axis=1), jnp.concatenate(weights, axis=1)

    def last_stage(h, dscore, weights, total_gain):
        cols = heads[h]
        keys = jnp.concatenate([fk_ref[:, cols], kv_ref[0, :, cols], near_ref[0, :, cols]], axis=0)
        vals = jnp.concatenate([fv_ref[:, cols], kv_ref[1, :, cols], near_ref[1, :, cols]], axis=0)
        grad_qn = dot(dscore, keys, NN) * scale
        out_ref[:, cols] = dot(weights, vals, NN).astype(BF16)
        key_t = dot(qt_ref[cols, :], dscore, NN) * scale
        own_ref[cols, :] = key_t[:, rows : 2 * rows].astype(BF16)
        to_far_ref[cols, :] = key_t[:, :rows].astype(BF16)
        to_near_ref[cols, :] = key_t[:, 2 * rows :].astype(BF16)
        unit = unit_ref[:, cols]
        product = grad_qn * unit
        mean = jnp.mean(product * q_gain, axis=1, keepdims=True)
        qgrad_ref[:, cols] = ((grad_qn * q_gain - unit * mean) * inverse_ref[:, cols]).astype(BF16)
        if h % GROUP == GROUP - 1:
            i = h // GROUP
            span = slice(heads[h - GROUP + 1].start, cols.stop)
            pairs = [
                (to_far_ref.at[span, :], far_hbm.at[0, span, :]),
                (to_near_ref.at[span, :], near_hbm.at[0, span, :]),
                (out_ref.at[:, span], out_hbm.at[:, span]),
                (qgrad_ref.at[:, span], qgrad_hbm.at[:, span]),
            ]
            for j, (here, there) in enumerate(pairs):
                copy = pltpu.make_async_copy(here, there, sems.at[i, j])
                copy.start()
                copies.append(copy)
        return total_gain + product

    total_gain = jnp.zeros((rows, width), F32)
    ahead = first_stage(0)
    behind = None
    for h in range(count):
        now = ahead
        if h + 1 < count:
            ahead = first_stage(h + 1)
        now = middle_stage(h, *now)
        if behind is not None:
            total_gain = last_stage(h - 1, *behind, total_gain)
        behind = now
    total_gain = last_stage(count - 1, *behind, total_gain)
    sums = jnp.sum(total_gain, axis=0, keepdims=True)
    spread_ref[...] = jnp.broadcast_to(sums[None], spread_ref.shape)
    copies.append(pltpu.make_async_copy(spread_ref, spread_hbm, sems.at[count // GROUP, 0]))
    copies[-1].start()
    for copy in copies:
        copy.wait()


def finish_kernel(
    kt_ref, own_k_ref, own_v_ref, far_ref, near_ref, gain_ref, kgrad_hbm, vgrad_hbm, inverse_ref, kgrad_ref, vgrad_ref, sems
):
    width = gain_ref.shape[1]
    row = gain_ref[...]
    inverse_ref[...] = 1.0 / row
    line = lax.broadcasted_iota(jnp.int32, (width, width), 0)
    diagonal = line == lax.broadcasted_iota(jnp.int32, (width, width), 1)
    gain = jnp.sum(jnp.where(diagonal, jnp.broadcast_to(row, (width, width)), 0.0), axis=1, keepdims=True)
    heads = head_columns(kgrad_ref, width)
    copies = []
    for h, cols in enumerate(heads):

        def total(i):
            own = (own_k_ref, own_v_ref)[i][cols, :].astype(F32)
            return own + far_ref[i, cols, :].astype(F32) + near_ref[i, cols, :].astype(F32)

        k = kt_ref[cols, :].astype(F32)
        inverse = inverse_spread(k, 0)
        unit = k * inverse
        scaled = total(0) * gain
        mean = jnp.mean(scaled * unit, axis=0, keepdims=True)
        kgrad_ref[:, cols] = ((scaled - unit * mean) * inverse).astype(BF16).T
        vgrad_ref[:, cols] = total(1).astype(BF16).T
        if h % STEP == STEP - 1:
            i = h // STEP
            span = slice(heads[h - STEP + 1].start, cols.stop)
            for j, (here, there) in enumerate([(kgrad_ref, kgrad_hbm), (vgrad_ref, vgrad_hbm)]):
                copies.append(pltpu.make_async_copy(here.at[:, span], there.at[:, span], sems.at[i, j]))
                copies[-1].start()
    for copy in copies:
        copy.wait()


def combine_kernel(parts_ref, spread_ref):
    spread_ref[...] = jnp.broadcast_to(jnp.sum(parts_ref[...], axis=0, keepdims=True), spread_ref.shape)


def gain_kernel(parts_ref, q_ref, inverse_ref, qgain_ref, kgain_ref):
    total = jnp.sum(parts_ref[...], axis=0)
    qgain_ref[...] = total
    kgain_ref[...] = total * q_ref[...] * inverse_ref[...]


def call(body, out_shape, flops, in_specs=None, out_specs=None, scratch=(), vmem=24):
    whole = pl.BlockSpec(memory_space=pltpu.VMEM)

    def run(*args):
        return pl.pallas_call(
            body,
            in_specs=in_specs or [whole] * len(args),
            out_specs=out_specs or [whole] * len(out_shape),
            out_shape=out_shape,
            scratch_shapes=scratch,
            compiler_params=pltpu.CompilerParams(vmem_limit_bytes=vmem * 1024 * 1024),
            cost_estimate=pl.CostEstimate(flops=flops, bytes_accessed=4 << 20, transcendentals=0),
        )(*args)

    return run


def exchange(parts, axis):
    return lax.all_to_all(parts, axis, 0, 0)


def shards(q_raw, k_raw, values, d_out, q_gain, k_gain, offsets, counts):
    rows, columns = q_raw.shape[1:]
    width = q_gain.shape[0]
    heads = offsets.shape[0]
    q, k, v, g = q_raw[0], k_raw[0], values[0], d_out[0]
    q_row, k_row = q_gain[None], k_gain[None]

    def like(*shape, dtype=BF16):
        return jax.ShapeDtypeStruct(shape, dtype)

    def far_away(shape):
        return pltpu.HBM(shape.shape, shape.dtype)

    hbm = pl.BlockSpec(memory_space=pltpu.HBM)
    vmem = pl.BlockSpec(memory_space=pltpu.VMEM)
    products = 2 * rows * rows * columns
    flat = like(rows, columns)
    turned = like(columns, rows)
    part = like(2, columns, rows)

    far_k, far_v = swap(k, 1), swap(v, 1)
    (identity,) = call(identity_kernel, [like(width, width, dtype=F32)], IDLE)()
    wide = like(rows, columns, dtype=F32)
    qn, qt, gt, kv, kt, unit, inverse, terms, mask = call(
        prepare_kernel,
        [flat, turned, turned, like(2, rows, columns), turned, wide, wide]
        + [like(2, rows, columns, dtype=F32), like(rows // TILE, heads, 3 * rows, dtype=F32)],
        2 * products,
    )(q, k, v, g, offsets.T, counts.T, identity, q_row, k_row)
    near = swap(kv, 0)
    (far_k,) = call(far_kernel, [flat], 2 * IDLE)(far_k, k_row)
    probs, dprob, far_v_part, own_v_part, near_v_part = call(
        side_kernel,
        [like(3, rows, columns, dtype=F32), wide, turned, turned, turned],
        6 * products,
    )(qn, g, gt, near, far_k, mask, terms)
    spread_one = like(lax.axis_size("seq"), 1, width, dtype=F32)
    out, q_grad, own_k_part, to_far, to_near, spread = call(
        attend_kernel,
        [far_away(flat), far_away(flat), turned, far_away(part), far_away(part), far_away(spread_one)],
        11 * products,
        out_specs=[hbm, hbm, vmem, hbm, hbm, hbm],
        scratch=[
            pltpu.VMEM((rows, columns), BF16),
            pltpu.VMEM((rows, columns), BF16),
            pltpu.VMEM((columns, rows), BF16),
            pltpu.VMEM((columns, rows), BF16),
            pltpu.VMEM(spread_one.shape, F32),
            pltpu.SemaphoreType.DMA((heads // GROUP + 1, 4)),
        ],
    )(g, qt, kv, near, far_k, far_v, probs, dprob, far_v_part, near_v_part, unit, inverse, terms, q_row)
    from_far = swap(to_far, 1)
    from_near = swap(to_near, 0)
    k_grad, v_grad, inverse_gain = call(
        finish_kernel,
        [far_away(flat), far_away(flat), like(1, width, dtype=F32)],
        rows * columns * 40,
        out_specs=[hbm, hbm, vmem],
        scratch=[
            pltpu.VMEM((rows, columns), BF16),
            pltpu.VMEM((rows, columns), BF16),
            pltpu.SemaphoreType.DMA((heads // STEP, 2)),
        ],
    )(kt, own_k_part, own_v_part, from_far, from_near, k_row)
    spread_two = like(lax.axis_size("dp"), 1, width, dtype=F32)
    (spread,) = call(combine_kernel, [spread_two], COMBINE)(exchange(spread, "seq"))
    parts = exchange(spread, "dp")
    gains = [like(1, width, dtype=F32)] * 2
    q_gain_grad, k_gain_grad = call(gain_kernel, gains, 0)(parts, q_row, inverse_gain)
    return (
        out[None],
        q_grad[None],
        k_grad[None],
        v_grad[None],
        q_gain_grad[0],
        k_gain_grad[0],
    )


def solution(mesh):
    tokens = P("dp", "seq", None)
    return jax.shard_map(
        shards,
        mesh=mesh,
        in_specs=(tokens, tokens, tokens, tokens, P(), P(), P(), P()),
        out_specs=(tokens, tokens, tokens, tokens, P(), P()),
        check_vma=False,
    )
```

```python
import math

import jax
import jax.numpy as jnp
from jax import lax
from jax.experimental import pallas as pl
from jax.experimental.pallas import tpu as pltpu
from jax.sharding import PartitionSpec as P

TILE = 64
REACH = 2
EPS = 1e-06
GROUP = 6
STEP = 6
IDLE = 5 * 10**9
COMBINE = 30 * 10**9
NT = (((1,), (1,)), ((), ()))
NN = (((1,), (0,)), ((), ()))
F32 = jnp.float32
BF16 = jnp.bfloat16


def dot(a, b, dims):
    return lax.dot_general(a, b, dims, preferred_element_type=F32)


def inverse_spread(rows, axis):
    return lax.rsqrt(jnp.mean(rows * rows, axis=axis, keepdims=True) + EPS)


def swap(block, parity):
    size = lax.axis_size("seq")
    route = [(i, i + 1 if i % 2 == parity else i - 1) for i in range(size)]
    return lax.ppermute(block, "seq", [(i, j) for i, j in route if 0 <= j < size])


def head_columns(ref, width):
    return [slice(h * width, (h + 1) * width) for h in range(ref.shape[-1] // width)]


def window_mask(offsets_t, counts_t, identity, position, t, rows):
    slots, heads = offsets_t.shape
    ntiles = counts_t.shape[1]
    tiles = rows // TILE
    lane = lax.broadcasted_iota(jnp.int32, (heads, 3 * rows), 1)
    side = 1 - 2 * lax.rem(position, 2)
    block = (lax.div(lane, rows) - 1) * side
    slot = block * tiles + lax.div(lax.rem(lane, rows), TILE) - t + REACH
    rank = jnp.zeros((heads, 3 * rows), F32)
    for s in range(slots):
        row = jnp.broadcast_to(offsets_t[s : s + 1, :], (heads, heads)).astype(F32)
        own = jnp.sum(row * identity, axis=1, keepdims=True)
        rank = rank + jnp.where(own == slot.astype(F32), float(s), 0.0)
    here = position * tiles + t
    tile = lax.broadcasted_iota(jnp.int32, (heads, ntiles), 1)
    used = jnp.sum(jnp.where(tile == here, counts_t.astype(F32), 0.0), axis=1, keepdims=True)
    key = here + slot - REACH
    inside = (slot >= 0) & (slot < slots) & (key >= 0) & (key < ntiles)
    return jnp.where(inside & ((slot == REACH) | (rank < used)), 1.0, 0.0)


def masked_terms(scores, scale, mask_ref, h, first):
    rows, wide = scores.shape
    mask = jnp.concatenate(
        [
            jnp.broadcast_to(mask_ref[t, h : h + 1, first : first + wide], (TILE, wide))
            for t in range(rows // TILE)
        ],
        axis=0,
    )
    return jnp.exp2(scores * (scale * math.log2(math.e))) * mask


def normal(raw, gain):
    rows = raw.astype(F32)
    return (rows * inverse_spread(rows, 1) * gain).astype(BF16)


def identity_kernel(identity_ref):
    size = identity_ref.shape[0]
    line = lax.broadcasted_iota(jnp.int32, (size, size), 0)
    identity_ref[...] = jnp.where(line == lax.broadcasted_iota(jnp.int32, (size, size), 1), 1.0, 0.0)


def prepare_kernel(
    q_ref, k_ref, v_ref, g_ref, offsets_ref, counts_ref, identity_ref, qgain_ref, kgain_ref,
    qn_ref, qt_ref, gt_ref, kv_ref, kt_ref, unit_ref, inverse_ref, own_ref, mask_ref,
):
    width = qgain_ref.shape[1]
    rows = q_ref.shape[0]
    scale = width ** (-0.5)
    q_gain = qgain_ref[...]
    k_gain = kgain_ref[...]
    position = lax.axis_index("seq")
    heads = offsets_ref.shape[1]
    identity = identity_ref[:heads, :heads]
    for t in range(rows // TILE):
        mask_ref[t] = window_mask(offsets_ref[...], counts_ref[...], identity, position, t, rows)
    for h, cols in enumerate(head_columns(q_ref, width)):
        q = q_ref[:, cols].astype(F32)
        inverse = inverse_spread(q, 1)
        unit = q * inverse
        unit_ref[:, cols] = unit
        inverse_ref[:, cols] = jnp.broadcast_to(inverse, (rows, width))
        qn = (unit * q_gain).astype(BF16)
        qn_ref[:, cols] = qn
        qt_ref[cols, :] = qn.T
        grads = g_ref[:, cols]
        gt_ref[cols, :] = grads.T
        raw = k_ref[:, cols]
        kt_ref[cols, :] = raw.T
        kn = normal(raw, k_gain)
        vals = v_ref[:, cols]
        kv_ref[0, :, cols] = kn
        kv_ref[1, :, cols] = vals
        own_ref[0, :, cols] = masked_terms(dot(qn, kn, NT), scale, mask_ref, h, rows)
        own_ref[1, :, cols] = dot(grads, vals, NT)


def far_kernel(k_ref, gain_ref, kn_ref):
    gain = gain_ref[...]
    for cols in head_columns(k_ref, gain_ref.shape[1]):
        kn_ref[:, cols] = normal(k_ref[:, cols], gain)


def side_kernel(
    qn_ref, g_ref, gt_ref, near_ref, fk_ref, kv_ref, mask_ref, own_ref,
    probs_ref, dprob_ref, sum_ref, far_v_ref, own_v_ref, near_v_ref,
):
    rows = qn_ref.shape[0]
    width = gt_ref.shape[0] // mask_ref.shape[1]
    scale = width ** (-0.5)
    heads = head_columns(qn_ref, width)
    count = len(heads)

    def first_stage(h):
        cols = heads[h]
        return dot(qn_ref[:, cols], jnp.concatenate([fk_ref[:, cols], near_ref[0, :, cols]], axis=0), NT)

    def middle_stage(h, scores):
        cols = heads[h]
        terms = [
            masked_terms(scores[:, :rows], scale, mask_ref, h, 0),
            own_ref[0, :, cols],
            masked_terms(scores[:, rows:], scale, mask_ref, h, 2 * rows),
        ]
        inverse = 1.0 / jnp.sum(terms[0] + terms[1] + terms[2], axis=1, keepdims=True)
        probs = [term * inverse for term in terms]
        for i, p in enumerate(probs):
            probs_ref[i, :, cols] = p
        return jnp.concatenate([p.astype(BF16) for p in probs], axis=1)

    def last_stage(h, weights):
        cols = heads[h]
        dprob_ref[:, cols] = dot(g_ref[:, cols], near_ref[1, :, cols], NT)
        vals = jnp.concatenate([kv_ref[1, :, cols], near_ref[1, :, cols]], axis=0)
        sum_ref[:, cols] = dot(weights[:, rows:], vals, NN)
        val_t = dot(gt_ref[cols, :], weights, NN).astype(BF16)
        for i, ref in enumerate([far_v_ref, own_v_ref, near_v_ref]):
            ref[cols, :] = val_t[:, i * rows : (i + 1) * rows]

    ahead = first_stage(0)
    behind = None
    for h in range(count):
        now = ahead
        if h + 1 < count:
            ahead = first_stage(h + 1)
        now = middle_stage(h, now)
        if behind is not None:
            last_stage(h - 1, behind)
        behind = now
    last_stage(count - 1, behind)


def attend_kernel(
    g_ref, qt_ref, kv_ref, near_ref, fk_ref, fv_ref, probs_ref, dprob_ref, sum_ref, far_v_ref, near_v_ref,
    unit_ref, inverse_ref, terms_ref, qgain_ref,
    out_hbm, qgrad_hbm, own_ref, far_hbm, near_hbm, spread_hbm,
    out_ref, qgrad_ref, to_far_ref, to_near_ref, spread_ref, sems,
):
    width = qgain_ref.shape[1]
    rows = g_ref.shape[0]
    scale = width ** (-0.5)
    q_gain = qgain_ref[...]
    heads = head_columns(g_ref, width)
    count = len(heads)
    copies = [
        pltpu.make_async_copy(far_v_ref, far_hbm.at[1], sems.at[count // GROUP, 1]),
        pltpu.make_async_copy(near_v_ref, near_hbm.at[1], sems.at[count // GROUP, 2]),
    ]
    for copy in copies:
        copy.start()

    def first_stage(h):
        return (dot(g_ref[:, heads[h]], fv_ref[:, heads[h]], NT),)

    def middle_stage(h, dprob):
        cols = heads[h]
        probs = [probs_ref[i, :, cols] for i in range(3)]
        dprobs = [dprob, terms_ref[1, :, cols], dprob_ref[:, cols]]
        delta = jnp.sum(
            probs[0] * dprobs[0] + probs[1] * dprobs[1] + probs[2] * dprobs[2], axis=1, keepdims=True
        )
        dscore = [(p * (d - delta)).astype(BF16) for p, d in zip(probs, dprobs)]
        return jnp.concatenate(dscore, axis=1), probs[0].astype(BF16)

    def last_stage(h, dscore, far_weights, total_gain):
        cols = heads[h]
        keys = jnp.concatenate([fk_ref[:, cols], kv_ref[0, :, cols], near_ref[0, :, cols]], axis=0)
        grad_qn = dot(dscore, keys, NN) * scale
        out_ref[:, cols] = (sum_ref[:, cols] + dot(far_weights, fv_ref[:, cols], NN)).astype(BF16)
        key_t = dot(qt_ref[cols, :], dscore, NN) * scale
        own_ref[cols, :] = key_t[:, rows : 2 * rows].astype(BF16)
        to_far_ref[cols, :] = key_t[:, :rows].astype(BF16)
        to_near_ref[cols, :] = key_t[:, 2 * rows :].astype(BF16)
        unit = unit_ref[:, cols]
        product = grad_qn * unit
        mean = jnp.mean(product * q_gain, axis=1, keepdims=True)
        qgrad_ref[:, cols] = ((grad_qn * q_gain - unit * mean) * inverse_ref[:, cols]).astype(BF16)
        if h % GROUP == GROUP - 1:
            i = h // GROUP
            span = slice(heads[h - GROUP + 1].start, cols.stop)
            pairs = [
                (to_far_ref.at[span, :], far_hbm.at[0, span, :]),
                (to_near_ref.at[span, :], near_hbm.at[0, span, :]),
                (out_ref.at[:, span], out_hbm.at[:, span]),
                (qgrad_ref.at[:, span], qgrad_hbm.at[:, span]),
            ]
            for j, (here, there) in enumerate(pairs):
                copy = pltpu.make_async_copy(here, there, sems.at[i, j])
                copy.start()
                copies.append(copy)
        return total_gain + product

    total_gain = jnp.zeros((rows, width), F32)
    ahead = first_stage(0)
    behind = None
    for h in range(count):
        now = ahead
        if h + 1 < count:
            ahead = first_stage(h + 1)
        now = middle_stage(h, *now)
        if behind is not None:
            total_gain = last_stage(h - 1, *behind, total_gain)
        behind = now
    total_gain = last_stage(count - 1, *behind, total_gain)
    sums = jnp.sum(total_gain, axis=0, keepdims=True)
    spread_ref[...] = jnp.broadcast_to(sums[None], spread_ref.shape)
    copies.append(pltpu.make_async_copy(spread_ref, spread_hbm, sems.at[count // GROUP, 0]))
    copies[-1].start()
    for copy in copies:
        copy.wait()


def finish_kernel(
    kt_ref, own_k_ref, own_v_ref, far_ref, near_ref, gain_ref, kgrad_hbm, vgrad_hbm, inverse_ref, kgrad_ref, vgrad_ref, sems
):
    width = gain_ref.shape[1]
    row = gain_ref[...]
    inverse_ref[...] = 1.0 / row
    line = lax.broadcasted_iota(jnp.int32, (width, width), 0)
    diagonal = line == lax.broadcasted_iota(jnp.int32, (width, width), 1)
    gain = jnp.sum(jnp.where(diagonal, jnp.broadcast_to(row, (width, width)), 0.0), axis=1, keepdims=True)
    heads = head_columns(kgrad_ref, width)
    copies = []
    for h, cols in enumerate(heads):

        def total(i):
            own = (own_k_ref, own_v_ref)[i][cols, :].astype(F32)
            return own + far_ref[i, cols, :].astype(F32) + near_ref[i, cols, :].astype(F32)

        k = kt_ref[cols, :].astype(F32)
        inverse = inverse_spread(k, 0)
        unit = k * inverse
        scaled = total(0) * gain
        mean = jnp.mean(scaled * unit, axis=0, keepdims=True)
        kgrad_ref[:, cols] = ((scaled - unit * mean) * inverse).astype(BF16).T
        vgrad_ref[:, cols] = total(1).astype(BF16).T
        if h % STEP == STEP - 1:
            i = h // STEP
            span = slice(heads[h - STEP + 1].start, cols.stop)
            for j, (here, there) in enumerate([(kgrad_ref, kgrad_hbm), (vgrad_ref, vgrad_hbm)]):
                copies.append(pltpu.make_async_copy(here.at[:, span], there.at[:, span], sems.at[i, j]))
                copies[-1].start()
    for copy in copies:
        copy.wait()


def combine_kernel(parts_ref, spread_ref):
    spread_ref[...] = jnp.broadcast_to(jnp.sum(parts_ref[...], axis=0, keepdims=True), spread_ref.shape)


def gain_kernel(parts_ref, q_ref, inverse_ref, qgain_ref, kgain_ref):
    total = jnp.sum(parts_ref[...], axis=0)
    qgain_ref[...] = total
    kgain_ref[...] = total * q_ref[...] * inverse_ref[...]


def call(body, out_shape, flops, in_specs=None, out_specs=None, scratch=(), vmem=24):
    whole = pl.BlockSpec(memory_space=pltpu.VMEM)

    def run(*args):
        return pl.pallas_call(
            body,
            in_specs=in_specs or [whole] * len(args),
            out_specs=out_specs or [whole] * len(out_shape),
            out_shape=out_shape,
            scratch_shapes=scratch,
            compiler_params=pltpu.CompilerParams(vmem_limit_bytes=vmem * 1024 * 1024),
            cost_estimate=pl.CostEstimate(flops=flops, bytes_accessed=4 << 20, transcendentals=0),
        )(*args)

    return run


def exchange(parts, axis):
    return lax.all_to_all(parts, axis, 0, 0)


def shards(q_raw, k_raw, values, d_out, q_gain, k_gain, offsets, counts):
    rows, columns = q_raw.shape[1:]
    width = q_gain.shape[0]
    heads = offsets.shape[0]
    q, k, v, g = q_raw[0], k_raw[0], values[0], d_out[0]
    q_row, k_row = q_gain[None], k_gain[None]

    def like(*shape, dtype=BF16):
        return jax.ShapeDtypeStruct(shape, dtype)

    def far_away(shape):
        return pltpu.HBM(shape.shape, shape.dtype)

    hbm = pl.BlockSpec(memory_space=pltpu.HBM)
    vmem = pl.BlockSpec(memory_space=pltpu.VMEM)
    products = 2 * rows * rows * columns
    flat = like(rows, columns)
    turned = like(columns, rows)
    part = like(2, columns, rows)

    far_k, far_v = swap(k, 1), swap(v, 1)
    (identity,) = call(identity_kernel, [like(width, width, dtype=F32)], IDLE)()
    wide = like(rows, columns, dtype=F32)
    qn, qt, gt, kv, kt, unit, inverse, terms, mask = call(
        prepare_kernel,
        [flat, turned, turned, like(2, rows, columns), turned, wide, wide]
        + [like(2, rows, columns, dtype=F32), like(rows // TILE, heads, 3 * rows, dtype=F32)],
        2 * products,
    )(q, k, v, g, offsets.T, counts.T, identity, q_row, k_row)
    near = swap(kv, 0)
    (far_k,) = call(far_kernel, [flat], 2 * IDLE)(far_k, k_row)
    probs, dprob, near_sum, far_v_part, own_v_part, near_v_part = call(
        side_kernel,
        [like(3, rows, columns, dtype=F32), wide, wide, turned, turned, turned],
        6 * products,
    )(qn, g, gt, near, far_k, kv, mask, terms)
    spread_one = like(lax.axis_size("seq"), 1, width, dtype=F32)
    out, q_grad, own_k_part, to_far, to_near, spread = call(
        attend_kernel,
        [far_away(flat), far_away(flat), turned, far_away(part), far_away(part), far_away(spread_one)],
        11 * products,
        out_specs=[hbm, hbm, vmem, hbm, hbm, hbm],
        scratch=[
            pltpu.VMEM((rows, columns), BF16),
            pltpu.VMEM((rows, columns), BF16),
            pltpu.VMEM((columns, rows), BF16),
            pltpu.VMEM((columns, rows), BF16),
            pltpu.VMEM(spread_one.shape, F32),
            pltpu.SemaphoreType.DMA((heads // GROUP + 1, 4)),
        ],
    )(g, qt, kv, near, far_k, far_v, probs, dprob, near_sum, far_v_part, near_v_part, unit, inverse, terms, q_row)
    from_far = swap(to_far, 1)
    from_near = swap(to_near, 0)
    k_grad, v_grad, inverse_gain = call(
        finish_kernel,
        [far_away(flat), far_away(flat), like(1, width, dtype=F32)],
        rows * columns * 40,
        out_specs=[hbm, hbm, vmem],
        scratch=[
            pltpu.VMEM((rows, columns), BF16),
            pltpu.VMEM((rows, columns), BF16),
            pltpu.SemaphoreType.DMA((heads // STEP, 2)),
        ],
    )(kt, own_k_part, own_v_part, from_far, from_near, k_row)
    spread_two = like(lax.axis_size("dp"), 1, width, dtype=F32)
    (spread,) = call(combine_kernel, [spread_two], COMBINE)(exchange(spread, "seq"))
    parts = exchange(spread, "dp")
    gains = [like(1, width, dtype=F32)] * 2
    q_gain_grad, k_gain_grad = call(gain_kernel, gains, 0)(parts, q_row, inverse_gain)
    return (
        out[None],
        q_grad[None],
        k_grad[None],
        v_grad[None],
        q_gain_grad[0],
        k_gain_grad[0],
    )


def solution(mesh):
    tokens = P("dp", "seq", None)
    return jax.shard_map(
        shards,
        mesh=mesh,
        in_specs=(tokens, tokens, tokens, tokens, P(), P(), P(), P()),
        out_specs=(tokens, tokens, tokens, tokens, P(), P()),
        check_vma=False,
    )
```
